256 devices in a mesh: gx: 8 (over x, core), gy: 32 (over y, z).
Axes of the slice: x: 4, y: 4, z: 8, core: 2. Of those that a mesh axis runs over, the one named last changes fastest.
Arguments:
- positions: float32 [3, 131072], P(None, ('gx', 'gy')), may hold values from 0 to 1
- atom_features: float32 [64, 131072], P(None, ('gx', 'gy')), may hold values from -6 to 6
- pair_neighbor: int32 [8192, 128], P(('gx', 'gy')), may hold values from -1 to 4607, as said below
- offload_slot: int32 [256, 32], P(('gx', 'gy')), may hold values from 0 to 31, each once within a row
- w_center: float32 [64, 256], replicated, may hold values from -0.5 to 0.5
- w_neigh: float32 [64, 256], replicated, may hold values from -0.5 to 0.5
- w_radial: float32 [8, 256], replicated, may hold values from -2 to 2
- w_env: bfloat16 [2, 256, 64], replicated, may hold values from -0.375 to 0.375
- w_latent: bfloat16 [2, 448, 256], replicated, may hold values from -0.25 to 0.25
- w_out: float32 [256], replicated, may hold values from -0.375 to 0.375
Outputs:
- forces: float32 [3, 131072], P(None, ('gx', 'gy'))
- atom_energy: float32 [16384], P(('gx', 'gy'))
- pair_energy: float32 [8192, 128], P(('gx', 'gy'))
The draws below stay inside these ranges and needn't reach their ends.
Inputs may be any that keep to these rules, and one draw needn't show every extreme that they name: `pair_neighbor`: row b of a device holds the neighbour lists of its atoms 2 * b and 2 * b + 1 in slots 0 to 63 and 64 to 127. Each list has its entries first and -1 after them; an entry n >= 0 names atom n % 512 of the domain at offset (n // 512 // 3 - 1, n // 512 % 3 - 1) along (gx, gy), never the centre itself. A list holds 2 to 64 entries, and some atom of every device has 64. Each device's row is a permutation; row b goes to the device with gy index offload_slot[b] // 1 and the same gx index.
All inputs are finite; a program needn't handle non-finite values.
Results may differ from the reference program's by a relative error of at most 0.008.
Values sent between devices are 32-bit elements; how exact they have to be, the bound alone decides.
No kernel may reach another device: no remote copies, remote signals or barrier semaphores. Data moves between devices by JAX's collectives and lax.ppermute only.
A program may use at most 64 MiB of HBM per device.

```python
import math
import jax
import jax.numpy as jnp
from jax import lax

ROWS_DEV = 32
ATOMS_DEV = 512
SLOTS = 64
FEATURES = 64
LATENT = 256
CHANNELS = 64
BASIS = 8
LAYERS = 2
PER_PEER = 1
ATOMS = 131072
ROWS = 8192
N_GX = 8
N_GY = 32


def draw_pair_neighbor(key, part):
    key = jax.random.fold_in(key, 11)
    key_low, key_count, key_full, key_pick = jax.random.split(key, 4)
    domains = N_GX * N_GY
    centre_count = 2 * ROWS_DEV
    low_count = jax.random.randint(key_low, (domains, 1), 2, SLOTS // 2 + 1)
    live_count = jax.random.randint(key_count, (domains, centre_count), low_count, SLOTS + 1)
    full_slot = jax.random.randint(key_full, (domains, 1), 0, centre_count)
    live_count = jnp.where(jnp.arange(centre_count)[None, :] == full_slot, SLOTS, live_count)
    chosen = jax.random.randint(key_pick, (domains, centre_count, SLOTS), 0, 9 * ATOMS_DEV - 1)
    self_index = 4 * ATOMS_DEV + jnp.arange(centre_count)[None, :, None]
    chosen = chosen + (chosen >= self_index).astype(jnp.int32)
    is_live = jnp.arange(SLOTS)[None, None, :] < live_count[:, :, None]
    listing = jnp.where(is_live, chosen, -1)
    return listing.reshape(domains * ROWS_DEV, 2 * SLOTS).astype(jnp.int32)


def block_scale(stream_key, extent, shards, least, high):
    level, own = 1.0, jax.random.fold_in(stream_key, 6)
    for axis_at, blocks in shards:
        steps = jnp.exp(jax.random.uniform(jax.random.fold_in(own, axis_at), (blocks,), jnp.float32, least / len(shards), high / len(shards)))
        level = level * jnp.repeat(steps, extent[axis_at] // blocks).reshape([-1 if axis == axis_at else 1 for axis in range(len(extent))])
    return level


def noise(key, shape, scale, limit, cuts=(), kind=jnp.bfloat16):
    values = scale * jax.random.normal(key, shape, jnp.float32)
    if cuts:
        values = values * block_scale(key, shape, cuts, -0.22, 0.18)
    return jnp.clip(values, -limit, limit).astype(kind)


def setup_inputs(seed: int = 0) -> dict:
    splits = jax.random.split(jax.random.key(seed), 11)
    positions = jnp.clip(1.0 * jax.random.uniform(splits[0], (3, ATOMS), jnp.float32) ** block_scale(splits[0], (3, ATOMS), ((1, 256),), -0.2, 0.2), 0.0, 1.0)
    atom_features = noise(splits[1], (FEATURES, ATOMS), 1.0, 6.0, ((1, 256),), jnp.float32)
    pair_neighbor = draw_pair_neighbor(jax.random.fold_in(splits[10], 71), 0)
    offload_slot = jax.vmap(lambda own: jax.random.permutation(own, ROWS_DEV))(jax.random.split(splits[3], (N_GX * N_GY))).reshape((N_GX * N_GY, ROWS_DEV)).astype(jnp.int32)
    w_center = noise(splits[4], (FEATURES, LATENT), (2 * FEATURES) ** -0.5, 0.5, (), jnp.float32)
    w_neigh = noise(splits[5], (FEATURES, LATENT), (2 * FEATURES) ** -0.5, 0.5, (), jnp.float32)
    w_radial = noise(splits[6], (BASIS, LATENT), BASIS ** -0.5, 2.0, (), jnp.float32)
    w_env = noise(splits[7], (LAYERS, LATENT, CHANNELS), LATENT ** -0.5, 0.375)
    w_latent = noise(splits[8], (LAYERS, LATENT + 3 * CHANNELS, LATENT), (LATENT + 3 * CHANNELS) ** -0.5, 0.25)
    w_out = noise(splits[9], (LATENT,), LATENT ** -0.5, 0.375, (), jnp.float32)
    return {"positions": positions, "atom_features": atom_features, "pair_neighbor": pair_neighbor, "offload_slot": offload_slot, "w_center": w_center, "w_neigh": w_neigh, "w_radial": w_radial, "w_env": w_env, "w_latent": w_latent, "w_out": w_out}


SOFTEN = 0.04
CUTOFF = 4.0

def harmonics(direction):
    comp_x, comp_y, comp_z = (direction[0], direction[1], direction[2])
    root_three = math.sqrt(3.0)
    root_five = math.sqrt(5.0)
    root_fifteen = math.sqrt(15.0)
    return jnp.stack([jnp.ones_like(comp_x), root_three * comp_x, root_three * comp_y, root_three * comp_z, root_fifteen * comp_x * comp_y, root_fifteen * comp_y * comp_z, 0.5 * root_five * (3.0 * comp_z * comp_z - 1.0), root_fifteen * comp_x * comp_z, 0.5 * root_fifteen * (comp_x * comp_x - comp_y * comp_y)])

def pair_energies(vectors, centre, neighbor_feat, validity, weights):
    w_center, w_neigh, w_radial, w_env, w_latent, w_out = weights
    nblocks, row_width = validity.shape
    slot_count = row_width // 2
    channels = w_env.shape[2]
    highest = lax.Precision.HIGHEST
    distance = jnp.sqrt(lax.optimization_barrier(jnp.sum(vectors * vectors, axis=0)) + SOFTEN)
    direction = vectors / distance
    scaled = distance / CUTOFF
    envelope = validity * jnp.square(1.0 - scaled * scaled)
    orders = jnp.arange(1, w_radial.shape[0] + 1, dtype=jnp.float32)
    radial_basis = jnp.sin(orders[:, None, None] * (jnp.pi * scaled)[None]) / distance[None]
    centre_part = jnp.einsum('fl,fbt->lbt', w_center, centre, precision=highest)
    centre_part = jnp.repeat(centre_part, slot_count, axis=2)
    preact = centre_part + jnp.einsum('fl,fbp->lbp', w_neigh, neighbor_feat, precision=highest)
    preact = preact + jnp.einsum('nl,nbp->lbp', w_radial, radial_basis, precision=highest)
    latent = jax.nn.silu(preact) * envelope
    harmonic = harmonics(direction)
    layer_count = w_env.shape[0]
    tensor = None
    for layer_index in range(layer_count):
        rounded = latent.astype(jnp.bfloat16)
        weight = jnp.einsum('lc,lbp->cbp', w_env[layer_index].astype(jnp.float32), rounded.astype(jnp.float32)) * envelope
        product = harmonic[:, None] * weight[None]
        environ = lax.optimization_barrier(jnp.sum(product.reshape(9, channels, nblocks, 2, slot_count), axis=-1)) / slot_count
        spread = jnp.repeat(environ, slot_count, axis=-1)
        if tensor is None:
            tensor = product
        paired = tensor * spread
        scalars = jnp.concatenate([paired[0], lax.optimization_barrier(jnp.sum(paired[1:4], axis=0)), lax.optimization_barrier(jnp.sum(paired[4:], axis=0))], axis=0)
        joined = jnp.concatenate([latent, scalars], axis=0).astype(jnp.bfloat16)
        update = jnp.einsum('kl,kbp->lbp', w_latent[layer_index].astype(jnp.float32), joined.astype(jnp.float32))
        latent = latent + jax.nn.silu(update)
        if layer_index + 1 < layer_count:
            tensor = tensor[0:1] * spread + spread[0:1] * tensor
    return jnp.einsum('l,lbp->bp', w_out, latent, precision=highest) * envelope

def reference(positions, atom_features, pair_neighbor, offload_slot, w_center, w_neigh, w_radial, w_env, w_latent, w_out):
    weights = (w_center, w_neigh, w_radial, w_env, w_latent, w_out)
    domains = N_GX * N_GY
    width_all = 3 + FEATURES
    atom_table = jnp.concatenate([positions, atom_features], axis=0).reshape(width_all, N_GX, N_GY, ATOMS_DEV)
    pieces = []
    for offset_x in range(3):
        for offset_y in range(3):
            moved = jnp.roll(atom_table, (1 - offset_x, 1 - offset_y), axis=(1, 2))
            moved = jnp.concatenate([moved[0:1] + (offset_x - 1.0), moved[1:2] + (offset_y - 1.0), moved[2:]], axis=0)
            pieces.append(moved)
    extended = jnp.stack(pieces, axis=1)
    extended = jnp.transpose(extended, (2, 3, 0, 1, 4)).reshape(domains, width_all, 9 * ATOMS_DEV)
    neighbours = pair_neighbor.reshape(domains, ROWS_DEV, 2 * SLOTS)

    def device_terms(inputs):
        ext_all, neighbor = inputs
        ext_pos = ext_all[:3]
        ext_feat = ext_all[3:]
        validity = (neighbor >= 0).astype(jnp.float32)
        neighbor_index = jnp.maximum(neighbor, 0)
        centres = 2 * jnp.arange(ROWS_DEV, dtype=jnp.int32)[:, None] + jnp.arange(2 * SLOTS, dtype=jnp.int32)[None, :] // SLOTS
        centre_index = 4 * ATOMS_DEV + 2 * jnp.arange(ROWS_DEV, dtype=jnp.int32)[:, None] + jnp.arange(2, dtype=jnp.int32)[None, :]
        centre = ext_feat[:, centre_index]
        neighbor_feat = ext_feat[:, neighbor_index]

        def energy_of(position_table):
            vectors = position_table[:, neighbor_index] - position_table[:, 4 * ATOMS_DEV + centres]
            return pair_energies(vectors, centre, neighbor_feat, validity, weights)
        energies, pullback = jax.vjp(energy_of, ext_pos)
        return (energies, pullback(jnp.ones_like(energies))[0])
    energies, gradients = lax.map(device_terms, (extended, neighbours))
    gradients = gradients.reshape(N_GX, N_GY, 3, 3, 3, ATOMS_DEV)
    total = jnp.zeros((N_GX, N_GY, 3, ATOMS_DEV), jnp.float32)
    for offset_x in range(3):
        for offset_y in range(3):
            total = total + jnp.roll(gradients[:, :, :, offset_x, offset_y], (offset_x - 1, offset_y - 1), axis=(0, 1))
    forces = -jnp.transpose(total, (2, 0, 1, 3)).reshape(3, ATOMS)
    atom_energy = energies.reshape(domains, ROWS_DEV, 2, SLOTS).sum(axis=-1).reshape(2 * ROWS)

    def place_rows(values, order):
        return jnp.zeros_like(values).at[order].set(values)
    placed = jax.vmap(place_rows)(energies, offload_slot)
    placed = placed.reshape(N_GX, N_GY, N_GY, PER_PEER, 2 * SLOTS)
    pair_energy = jnp.transpose(placed, (0, 2, 1, 3, 4)).reshape(ROWS, 2 * SLOTS)
    return (forces, atom_energy, pair_energy)
```

```python
import math

import jax
import jax.numpy as jnp
from jax import lax
from jax.experimental import pallas as pl
from jax.experimental.pallas import tpu as pltpu
from jax.sharding import PartitionSpec as P

SOFTEN = 0.04
CUTOFF = 4.0
BF = jnp.bfloat16
F32 = jnp.float32
R3 = math.sqrt(3.0)
R5 = math.sqrt(5.0)
R15 = math.sqrt(15.0)
ROWS = 32
WIDTH = 128
SLOTS = 64
ATOMS = 512
NB = 8
M = NB * WIDTH
NT = (((1,), (1,)), ((), ()))
HPAD = 40


def mm(a, b):
    return jnp.dot(a, b, preferred_element_type=F32)


def cat(*xs):
    return jnp.concatenate(xs, axis=1)


def mm_nt(a, b):
    return lax.dot_general(a, b, NT, preferred_element_type=F32)


def split2(x):
    hi = x.astype(BF)
    return hi, (x - hi.astype(F32)).astype(BF)


def kernel(
    idx_s, slot_s, idx_v, t0, t1, t2, t3, t4, t5, t6, t7, t8, cpart, win_ref,
    we0_ref, we1_ref, wl0_ref, wl1_ref, wl0t_ref, wl1t_ref, lat0t_ref, lat1t_ref,
    wout_ref, rad_ref,
    left_ref, mid_ref, right_ref, ae_ref, placed_ref,
    table, gbuf, pos, geo, bgeo, lhs, rhs,
):
    tables = (t0, t1, t2, t3, t4, t5, t6, t7, t8)
    feats = 64
    for o in range(9):
        ref = tables[o]
        shift = jnp.concatenate(
            [jnp.full((1, ATOMS), o // 3 - 1.0, F32), jnp.full((1, ATOMS), o % 3 - 1.0, F32),
             jnp.zeros((1, ATOMS), F32)], axis=0)
        posr = ref[feats:feats + 3, :] + shift
        for q in range(ATOMS // 128):
            block = jnp.concatenate(
                [ref[0:feats, q * 128:(q + 1) * 128], posr[:, q * 128:(q + 1) * 128],
                 jnp.zeros((61, 128), F32)], axis=0)
            table[pl.ds(o * ATOMS + q * 128, 128), :] = block.T

    def gather_row(b, carry):
        base = b * WIDTH
        for t in range(WIDTH):
            n = jnp.maximum(idx_s[b, t], 0)
            gbuf[pl.ds(base + t, 1), :] = table[pl.ds(n, 1), :]
        gt = gbuf[pl.ds(pl.multiple_of(base, WIDTH), WIDTH), :].T
        for c in range(3):
            pos[c, pl.ds(b, 1), :] = gt[feats + c:feats + c + 1, :]
        return carry

    lax.fori_loop(0, ROWS, gather_row, 0)

    lane = lax.broadcasted_iota(jnp.int32, (ROWS, WIDTH), 1)
    own = table[pl.ds(4 * ATOMS, 128), :]
    own_t = own.T
    row_i = lax.broadcasted_iota(jnp.int32, (ROWS, WIDTH), 0)
    vec = []
    for c in range(3):
        line = jnp.broadcast_to(own_t[feats + c:feats + c + 1, :], (ROWS, WIDTH))
        first = jnp.sum(jnp.where(lane == 2 * row_i, line, 0.0), axis=1, keepdims=True)
        second = jnp.sum(jnp.where(lane == 2 * row_i + 1, line, 0.0), axis=1, keepdims=True)
        vec.append(pos[c] - jnp.where(lane < SLOTS, first, second))
    vx, vy, vz = vec
    index = idx_v[...]
    valid = (index >= 0).astype(F32)
    dist = jnp.sqrt(vx * vx + vy * vy + vz * vz + SOFTEN)
    inv = 1.0 / dist
    ux, uy, uz = vx * inv, vy * inv, vz * inv
    scaled = dist * (1.0 / CUTOFF)
    poly = 1.0 - scaled * scaled
    env = valid * (poly * poly)
    theta = math.pi * scaled
    sin1, cos1 = jnp.sin(theta), jnp.cos(theta)
    sins, coss = [sin1], [cos1]
    sprev, cprev = jnp.zeros_like(sin1), jnp.ones_like(cos1)
    for _ in range(7):
        snext = 2.0 * cos1 * sins[-1] - sprev
        cnext = 2.0 * cos1 * coss[-1] - cprev
        sprev, cprev = sins[-1], coss[-1]
        sins.append(snext)
        coss.append(cnext)
    sph = [
        jnp.ones_like(ux), R3 * ux, R3 * uy, R3 * uz, R15 * ux * uy, R15 * uy * uz,
        0.5 * R5 * (3.0 * uz * uz - 1.0), R15 * ux * uz, 0.5 * R15 * (ux * ux - uy * uy),
    ]
    zero = jnp.zeros_like(ux)
    rows = sph + [zero] * 7
    for s in sins:
        rows.append(s * inv)
    rows.append(env)
    rows += [zero] * 7
    for q in range(len(rows)):
        for b in range(ROWS):
            geo[b, q:q + 1, :] = rows[q][b:b + 1, :]

    lane_b = lax.broadcasted_iota(jnp.int32, (16, WIDTH), 1)
    half0 = (lane_b < SLOTS).astype(F32)
    half1 = 1.0 - half0
    kk = lax.broadcasted_iota(jnp.int32, (32, 256), 0) % 16
    gg = lax.broadcasted_iota(jnp.int32, (32, 256), 1) // 64
    group = jnp.where(kk == 0, 0, jnp.where(kk < 4, 1, jnp.where(kk < 9, 2, 4)))
    gmask = (group == gg).astype(F32)
    row0 = (kk == 0).astype(F32)
    upper = (lax.broadcasted_iota(jnp.int32, (32, 128), 1) >= 64)
    upper_m = lax.broadcasted_iota(jnp.int32, (M, 128), 1) >= 64
    first_row = lax.broadcasted_iota(jnp.int32, (32, 1), 0) < 16

    def row0_of(x):
        return jnp.concatenate(
            [jnp.broadcast_to(x[0:1], (16, x.shape[1])), jnp.broadcast_to(x[16:17], (16, x.shape[1]))], axis=0)

    def ksum(x):
        s0 = jnp.sum(x[0:16], axis=0, keepdims=True)
        s1 = jnp.sum(x[16:32], axis=0, keepdims=True)
        return jnp.concatenate(
            [jnp.broadcast_to(s0, (16, x.shape[1])), jnp.broadcast_to(s1, (16, x.shape[1]))], axis=0) * row0

    def fold(x):
        s = x[:, 0:128] + x[:, 128:256]
        return s + pltpu.roll(s, 64, 1)

    def act(h):
        t = jnp.tanh(h)
        u = 1.0 + t
        a = h * u
        return a, u + a * (1.0 - t)

    def chunk(i, carry):
        first = pl.multiple_of(i * M, M)
        g = gbuf[pl.ds(first, M), :]
        ghi, glo = split2(g)
        st, tr, cadd = [], [], []
        centres = cpart[pl.ds(pl.multiple_of(i * 2 * NB, 2 * NB), 2 * NB), :]
        for b in range(NB):
            blk = geo[i * NB + b]
            s0 = blk[0:16] * half0
            s1 = blk[0:16] * half1
            bas = blk[16:24]
            bhi = bas.astype(BF).astype(F32)
            full = jnp.concatenate(
                [s0, s1, bhi, bas - bhi, bhi, blk[24:32], jnp.zeros((64, WIDTH), F32)], axis=0)
            tr.append(full.T)
            st.append(jnp.concatenate([s0, s1], axis=0).astype(BF))
            cadd.append(jnp.broadcast_to(centres[2 * b:2 * b + 1], (SLOTS, 256)))
            cadd.append(jnp.broadcast_to(centres[2 * b + 1:2 * b + 2], (SLOTS, 256)))
        trans = jnp.concatenate(tr, axis=0)
        env1 = jnp.broadcast_to(trans[:, 56:57], (M, 128))
        env2 = jnp.concatenate([env1, env1], axis=1)
        tb = trans.astype(BF)
        sbd = tb[:, 0:32]
        h0 = (
            mm(cat(ghi, glo, ghi, tb), win_ref[...])
            + jnp.concatenate(cadd, axis=0)
        )
        a0, d0 = act(h0)
        lat0 = a0 * env2
        r0 = lat0.astype(BF)
        y0 = mm(r0, we0_ref[...])
        w0 = y0 * env2
        w0b = w0.astype(BF)

        def per_row(fn):
            return [fn(b, slice(b * WIDTH, (b + 1) * WIDTH)) for b in range(NB)]

        e0 = per_row(lambda b, s: mm(st[b], w0b[s]) * (1.0 / SLOTS))
        b0 = [(e * gmask).astype(BF) for e in e0]
        a_0 = jnp.concatenate(per_row(lambda b, s: mm(sbd[s], b0[b])), axis=0)
        sc0 = (w0 * a_0).astype(BF)
        h1 = mm(cat(r0, sc0), wl0_ref[...])
        a1, d1 = act(h1)
        lat1 = lat0 + a1
        r1 = lat1.astype(BF)
        y1 = mm(r1, we1_ref[...])
        w1b = (y1 * env2).astype(BF)
        e1 = per_row(lambda b, s: mm(st[b], w1b[s]) * (1.0 / SLOTS))
        b1 = [row0_of(e0[b]) * e1[b] * gmask + ksum(e0[b] * e1[b] * gmask) for b in range(NB)]
        b1 = [x.astype(BF) for x in b1]
        a_1 = jnp.concatenate(per_row(lambda b, s: mm(sbd[s], b1[b])), axis=0)
        sc1 = (w0 * a_1).astype(BF)
        h2 = mm(cat(r1, sc1), wl1_ref[...])
        a2, d2 = act(h2)
        wo = wout_ref[...]
        pq = (lat1 + a2) * wo
        pqh, pql = split2(pq[:, 0:128] + pq[:, 128:256])
        dlat2 = env2 * wo
        dz1 = (dlat2 * d2).astype(BF)
        dsc1 = mm(dz1, wl1t_ref[...])
        dw0 = dsc1 * a_1
        da1 = dsc1 * w0
        da1 = jnp.concatenate(
            [da1[:, 0:128].astype(BF), jnp.where(upper_m, w1b[:, 128:256].astype(F32), da1[:, 128:256]).astype(BF)], axis=1)
        db1 = per_row(lambda b, s: mm(st[b], da1[s]))
        de1, x0 = [], []
        for b in range(NB):
            head = row0_of(db1[b])
            prod = db1[b] * gmask
            de1.append(fold(gmask * head * e0[b] + prod * row0_of(e0[b])) * (1.0 / SLOTS))
            x0.append(gmask * head * e1[b] + ksum(prod * e1[b]))
        de1 = [jnp.where(upper, x, 0.0).astype(BF) for x in de1]
        b1c = [jnp.concatenate([b1[b][:, 0:128], (b1[b][:, 128:256].astype(F32) + de1[b].astype(F32)).astype(BF)], axis=1) for b in range(NB)]
        ds1 = per_row(lambda b, s: mm_nt(da1[s], b1c[b]))
        dw1 = jnp.concatenate(per_row(lambda b, s: mm(sbd[s], de1[b])), axis=0)
        ev = dw1 * y1[:, 128:256]
        dlat1 = dlat2 + mm(cat(dz1, (dw1 * env1).astype(BF)), lat1t_ref[...])
        dz0 = (dlat1 * d1).astype(BF)
        dsc0 = mm(dz0, wl0t_ref[...])
        dw0 = dw0 + dsc0 * a_0
        da0 = dsc0 * w0
        da0 = jnp.concatenate(
            [da0[:, 0:128].astype(BF), jnp.where(upper_m, w0[:, 128:256], da0[:, 128:256]).astype(BF)], axis=1)
        db0 = per_row(lambda b, s: mm(st[b], da0[s]))
        de0 = [jnp.where(upper, fold(x0[b] + gmask * db0[b]) * (1.0 / SLOTS), 0.0) for b in range(NB)]
        b0c = [jnp.concatenate([b0[b][:, 0:128], (b0[b][:, 128:256].astype(F32) + de0[b]).astype(BF)], axis=1) for b in range(NB)]
        ds = per_row(lambda b, s: ds1[b] + mm_nt(da0[s], b0c[b]))
        dw0e = jnp.concatenate(per_row(lambda b, s: mm(sbd[s], de0[b].astype(BF))), axis=0)
        dw0 = jnp.concatenate([dw0[:, 0:128], dw0[:, 128:256] + dw0e], axis=1)
        dlat0 = dlat1 + mm(cat(dz0, (dw0 * env2).astype(BF)), lat0t_ref[...])
        evl = dlat0 * a0 + dw0 * y0
        ev = ev + evl[:, 0:128] + evl[:, 128:256]
        evh, evo = split2(ev)
        dx0 = (dlat0 * env2 * d0).astype(BF)
        res = mm(cat(dx0, pqh, pql, evh, evo), rad_ref[...])
        for b in range(NB):
            dst = ds[b].T
            bgeo[i * NB + b, 0:16, :] = dst[0:16] * half0 + dst[16:32] * half1
            bgeo[i * NB + b, 16:32, :] = res[b * WIDTH:(b + 1) * WIDTH].T[0:16]
        return carry

    lax.fori_loop(0, ROWS // NB, chunk, 0)

    back = []
    for q in range(26):
        back.append(jnp.concatenate([bgeo[b, q:q + 1, :] for b in range(ROWS)], axis=0))
    gs, gb, q_e, denv = back[0:9], back[16:24], back[24], back[25]
    energy = env * q_e
    denv = denv + q_e
    dux = R3 * gs[1] + R15 * (uy * gs[4] + uz * gs[7] + ux * gs[8])
    duy = R3 * gs[2] + R15 * (ux * gs[4] + uz * gs[5] - uy * gs[8])
    duz = R3 * gs[3] + R15 * (uy * gs[5] + ux * gs[7]) + 3.0 * R5 * uz * gs[6]
    dd = denv * (valid * poly * scaled * (-4.0 / CUTOFF))
    for n in range(8):
        dd = dd + gb[n] * inv * (((n + 1) * math.pi / CUTOFF) * coss[n] - sins[n] * inv)
    dd = dd - (dux * ux + duy * uy + duz * uz) * inv
    dv = [dux * inv + dd * ux, duy * inv + dd * uy, duz * inv + dd * uz]

    safe = jnp.maximum(index, 0)
    nhi = safe // 128
    nlo = safe - nhi * 128
    sub_h = lax.broadcasted_iota(jnp.int32, (HPAD, WIDTH), 0)
    sub_l = lax.broadcasted_iota(jnp.int32, (128, WIDTH), 0)
    half_i = lax.broadcasted_iota(jnp.int32, (128, WIDTH), 1) // SLOTS
    ehi = energy.astype(BF).astype(F32)
    elo = energy - ehi
    dvh = [x.astype(BF).astype(F32) for x in dv]
    dvl = [x - y for x, y in zip(dv, dvh)]
    for b in range(ROWS):
        cols = slice(b * WIDTH, (b + 1) * WIDTH)
        pick = sub_h == nhi[b:b + 1]
        parts = [jnp.where(pick, x[b:b + 1], 0.0) for x in dvh + dvl]
        parts.append(jnp.where(lax.broadcasted_iota(jnp.int32, (16, WIDTH), 0) == 0, ehi[b:b + 1],
                               jnp.where(lax.broadcasted_iota(jnp.int32, (16, WIDTH), 0) == 1, elo[b:b + 1], 0.0)))
        lhs[:, cols] = jnp.concatenate(parts, axis=0).astype(BF)
        low = (sub_l == nlo[b:b + 1]).astype(F32)
        cen = (sub_l == 2 * b + half_i).astype(F32)
        rhs[:, cols] = jnp.concatenate([low, cen], axis=0).astype(BF)
        placed_ref[pl.ds(slot_s[0, b], 1), :] = energy[b:b + 1]
    acc = mm_nt(lhs[...], rhs[...])
    for c in range(3):
        both = acc[c * HPAD:(c + 1) * HPAD] + acc[(3 + c) * HPAD:(4 + c) * HPAD]
        centre = jnp.sum(both[:, 128:256], axis=0, keepdims=True)
        ghost = jnp.where(sub_h == 4 * 4, jnp.broadcast_to(centre, (HPAD, 128)), 0.0) - both[:, 0:128]
        left_ref[12 * c:12 * c + 12] = ghost[0:12]
        mid_ref[12 * c:12 * c + 12] = ghost[12:24]
        right_ref[12 * c:12 * c + 12] = ghost[24:36]
    ae_ref[...] = acc[240:241, 128:192] + acc[241:242, 128:192]


def local_terms(tables, pair_neighbor, offload_slot, cpart, weights):
    vm = pl.BlockSpec(memory_space=pltpu.VMEM)
    sm = pl.BlockSpec(memory_space=pltpu.SMEM)
    operands = [pair_neighbor, offload_slot, pair_neighbor, *tables, cpart, *weights]
    specs = [sm, sm] + [vm] * (len(operands) - 2)
    return pl.pallas_call(
        kernel,
        out_shape=[
            jax.ShapeDtypeStruct((36, 128), F32),
            jax.ShapeDtypeStruct((36, 128), F32),
            jax.ShapeDtypeStruct((36, 128), F32),
            jax.ShapeDtypeStruct((1, 64), F32),
            jax.ShapeDtypeStruct((ROWS, WIDTH), F32),
        ],
        in_specs=specs,
        out_specs=[vm] * 5,
        scratch_shapes=[
            pltpu.VMEM((9 * ATOMS, 128), F32),
            pltpu.VMEM((ROWS * WIDTH, 128), F32),
            pltpu.VMEM((3, ROWS, WIDTH), F32),
            pltpu.VMEM((ROWS, 32, WIDTH), F32),
            pltpu.VMEM((ROWS, 32, WIDTH), F32),
            pltpu.VMEM((256, ROWS * WIDTH), BF),
            pltpu.VMEM((256, ROWS * WIDTH), BF),
        ],
        compiler_params=pltpu.CompilerParams(vmem_limit_bytes=56 * 1024 * 1024),
    )(*operands)


def prepare(atom_features, w_center, w_neigh, w_radial, w_env, w_latent, w_out):
    highest = lax.Precision.HIGHEST
    cpart = 0.5 * jnp.einsum("fc,fl->cl", atom_features[:, : 2 * ROWS], w_center, precision=highest)
    wn = 0.5 * w_neigh
    wn_hi, wn_lo = split2(wn)
    wr = 0.5 * w_radial
    wr_hi, wr_lo = split2(wr)
    z64 = jnp.zeros((64, 256), BF)
    win = jnp.concatenate(
        [wn_hi, z64, wn_hi, z64, wn_lo, z64, jnp.zeros((32, 256), BF), wr_hi, wr_hi, wr_lo, jnp.zeros((72, 256), BF)], axis=0)
    we0 = jnp.tile(w_env[0], (1, 4))
    we1 = jnp.tile(w_env[1], (1, 4))
    half = jnp.asarray(0.5, BF)
    pad = jnp.zeros((64, 256), BF)
    wl0 = jnp.concatenate([w_latent[0] * half, pad], axis=0)
    wl1 = jnp.concatenate([w_latent[1] * half, pad], axis=0)
    wl0t, wl1t = wl0.T, wl1.T
    lat0t = jnp.concatenate([wl0t[:, 0:256], we0.T], axis=0)
    lat1t = jnp.concatenate([wl1t[:, 0:256], we1.T[0:128]], axis=0)
    ones = jnp.ones((256, 1), BF)
    col = lambda j: jnp.pad(ones, ((0, 0), (j, 127 - j)))
    rad = jnp.pad(wr_hi.T, ((0, 0), (0, 120)))
    rad = jnp.concatenate([rad, col(8), col(9)], axis=0)
    return cpart, (win, we0, we1, wl0, wl1, wl0t[:, 256:512], wl1t[:, 256:512], lat0t, lat1t, w_out[None, :], rad)


def per_device(
    positions, atom_features, pair_neighbor, offload_slot,
    w_center, w_neigh, w_radial, w_env, w_latent, w_out,
):
    def shift(x, axis, step):
        n = lax.axis_size(axis)
        return lax.ppermute(x, axis, [(i, (i + step) % n) for i in range(n)])

    own = jnp.concatenate([atom_features, positions], axis=0)
    col = [shift(own, "gy", 1), own, shift(own, "gy", -1)]
    left = [None, shift(own, "gx", 1), None]
    right = [None, shift(own, "gx", -1), None]
    for oy in (0, 2):
        left[oy] = shift(col[oy], "gx", 1)
        right[oy] = shift(col[oy], "gx", -1)
    cpart, weights = prepare(atom_features, w_center, w_neigh, w_radial, w_env, w_latent, w_out)
    g_left, g_mid, g_right, ae, placed = local_terms(
        left + col + right, pair_neighbor, offload_slot, cpart, weights)
    from_left = shift(g_right, "gx", 1)
    from_right = shift(g_left, "gx", -1)
    peers = lax.axis_size("gy")
    pair_energy = lax.all_to_all(
        placed.reshape(peers, ROWS // peers, WIDTH), "gy", split_axis=0, concat_axis=0, tiled=True
    ).reshape(ROWS, WIDTH)
    total = (g_mid + from_left + from_right).reshape(3, 3, 4, 128)
    forces = total[:, 1] + shift(total[:, 2], "gy", 1) + shift(total[:, 0], "gy", -1)
    return forces.reshape(3, ATOMS), ae.reshape(2 * ROWS), pair_energy


def solution(mesh):
    spread = P(None, ("gx", "gy"))
    rows = P(("gx", "gy"), None)
    return jax.shard_map(
        per_device,
        mesh=mesh,
        in_specs=(spread, spread, rows, rows, P(), P(), P(), P(), P(), P()),
        out_specs=(spread, P(("gx", "gy")), rows),
        check_vma=False,
    )
```

```python
import math

import jax
import jax.numpy as jnp
from jax import lax
from jax.experimental import pallas as pl
from jax.experimental.pallas import tpu as pltpu
from jax.sharding import PartitionSpec as P

SOFTEN = 0.04
CUTOFF = 4.0
BF = jnp.bfloat16
F32 = jnp.float32
R3 = math.sqrt(3.0)
R5 = math.sqrt(5.0)
R15 = math.sqrt(15.0)
ROWS = 32
WIDTH = 128
SLOTS = 64
ATOMS = 512
NB = 8
M = NB * WIDTH
NT = (((1,), (1,)), ((), ()))
HPAD = 40
LEAD = 8


def mm(a, b):
    return jnp.dot(a, b, preferred_element_type=F32)


def cat(*xs):
    return jnp.concatenate(xs, axis=1)


def mm_nt(a, b):
    return lax.dot_general(a, b, NT, preferred_element_type=F32)


def split2(x):
    hi = x.astype(BF)
    return hi, (x - hi.astype(F32)).astype(BF)


def geometry(vx, vy, vz, index):
    valid = (index >= 0).astype(F32)
    dist = jnp.sqrt(vx * vx + vy * vy + vz * vz + SOFTEN)
    inv = 1.0 / dist
    scaled = dist * (1.0 / CUTOFF)
    poly = 1.0 - scaled * scaled
    env = valid * (poly * poly)
    theta = math.pi * scaled
    sins, coss = [jnp.sin(theta)], [jnp.cos(theta)]
    twice = 2.0 * coss[0]
    sprev, cprev = jnp.zeros_like(inv), jnp.ones_like(inv)
    for _ in range(7):
        snext = twice * sins[-1] - sprev
        cnext = twice * coss[-1] - cprev
        sprev, cprev = sins[-1], coss[-1]
        sins.append(snext)
        coss.append(cnext)
    return vx * inv, vy * inv, vz * inv, inv, valid, poly, scaled, env, sins, coss


def kernel(
    idx_s, slot_s, idx_v, t0, t1, t2, t3, t4, t5, t6, t7, t8, cpart, win_ref,
    we0_ref, we1_ref, wl0_ref, wl1_ref, wl0t_ref, wl1t_ref, lat0t_ref, lat1t_ref,
    rad_ref, wout_ref,
    terms_ref, placed_ref,
    table, gbuf, pos, geo, bgeo,
):
    tables = (t0, t1, t2, t3, t4, t5, t6, t7, t8)
    feats = 64
    table[0:LEAD, :] = jnp.zeros((LEAD, 128), F32)
    for o in range(9):
        ref = tables[o]
        shift = jnp.concatenate(
            [jnp.full((1, ATOMS), o // 3 - 1.0, F32), jnp.full((1, ATOMS), o % 3 - 1.0, F32),
             jnp.zeros((1, ATOMS), F32)], axis=0)
        posr = ref[feats:feats + 3, :] + shift
        for q in range(ATOMS // 128):
            block = jnp.concatenate(
                [ref[0:feats, q * 128:(q + 1) * 128], posr[:, q * 128:(q + 1) * 128],
                 jnp.zeros((61, 128), F32)], axis=0)
            table[pl.ds(LEAD + o * ATOMS + q * 128, 128), :] = block.T

    lane = lax.broadcasted_iota(jnp.int32, (NB, WIDTH), 1)
    row_i = lax.broadcasted_iota(jnp.int32, (NB, WIDTH), 0)
    own_t = table[pl.ds(LEAD + 4 * ATOMS, 128), :].T

    def stage(i):
        start = pl.multiple_of(i * M, M)
        for b in range(NB):
            for t in range(WIDTH):
                gbuf[pl.ds(start + (b * WIDTH + t), 1), :] = table[pl.ds(idx_s[i * NB + b, t] + LEAD, 1), :]
        turned = [gbuf[pl.ds(start + b * WIDTH, WIDTH), :].T for b in range(NB)]
        some = pl.ds(pl.multiple_of(i * NB, NB), NB)
        vec = []
        for c in range(3):
            end = jnp.concatenate([x[feats + c:feats + c + 1] for x in turned], axis=0)
            line = jnp.broadcast_to(own_t[feats + c:feats + c + 1, :], (NB, WIDTH))
            at = 2 * (row_i + i * NB)
            first = jnp.sum(jnp.where(lane == at, line, 0.0), axis=1, keepdims=True)
            second = jnp.sum(jnp.where(lane == at + 1, line, 0.0), axis=1, keepdims=True)
            vec.append(end - jnp.where(lane < SLOTS, first, second))
            pos[c, some, :] = vec[-1]
        ux, uy, uz, inv, _, _, _, env, sins, _ = geometry(*vec, idx_v[some, :])
        zero = jnp.zeros_like(ux)
        rows = [
            jnp.ones_like(ux), R3 * ux, R3 * uy, R3 * uz, R15 * ux * uy, R15 * uy * uz,
            0.5 * R5 * (3.0 * uz * uz - 1.0), R15 * ux * uz, 0.5 * R15 * (ux * ux - uy * uy),
        ] + [zero] * 7 + [x * inv for x in sins] + [env] + [zero] * 7
        for q in range(len(rows)):
            for b in range(NB):
                geo[i * NB + b, q:q + 1, :] = rows[q][b:b + 1, :]

    stage(0)

    lane_b = lax.broadcasted_iota(jnp.int32, (16, WIDTH), 1)
    half0 = (lane_b < SLOTS).astype(F32)
    half1 = 1.0 - half0
    kk = lax.broadcasted_iota(jnp.int32, (32, 256), 0) % 16
    gg = lax.broadcasted_iota(jnp.int32, (32, 256), 1) // 64
    group = jnp.where(kk == 0, 0, jnp.where(kk < 4, 1, jnp.where(kk < 9, 2, 4)))
    gmask = (group == gg).astype(F32)
    row0 = (kk == 0).astype(F32)
    upper = (lax.broadcasted_iota(jnp.int32, (32, 128), 1) >= 64)
    upper_m = lax.broadcasted_iota(jnp.int32, (M, 128), 1) >= 64
    first_row = lax.broadcasted_iota(jnp.int32, (32, 1), 0) < 16

    def row0_of(x):
        return jnp.concatenate(
            [jnp.broadcast_to(x[0:1], (16, x.shape[1])), jnp.broadcast_to(x[16:17], (16, x.shape[1]))], axis=0)

    def ksum(x):
        s0 = jnp.sum(x[0:16], axis=0, keepdims=True)
        s1 = jnp.sum(x[16:32], axis=0, keepdims=True)
        return jnp.concatenate(
            [jnp.broadcast_to(s0, (16, x.shape[1])), jnp.broadcast_to(s1, (16, x.shape[1]))], axis=0) * row0

    def fold(x):
        s = x[:, 0:128] + x[:, 128:256]
        return s + pltpu.roll(s, 64, 1)

    def act(h):
        t = jnp.tanh(h)
        u = 1.0 + t
        a = h * u
        return a, u + a * (1.0 - t)

    def chunk(i, carry):
        first = pl.multiple_of(i * M, M)
        g = gbuf[pl.ds(first, M), :]
        ghi, glo = split2(g)
        st, tr, cadd = [], [], []
        centres = cpart[pl.ds(pl.multiple_of(i * 2 * NB, 2 * NB), 2 * NB), :]
        for b in range(NB):
            blk = geo[i * NB + b]
            s0 = blk[0:16] * half0
            s1 = blk[0:16] * half1
            bas = blk[16:24]
            bhi = bas.astype(BF).astype(F32)
            full = jnp.concatenate(
                [s0, s1, bhi, bas - bhi, bhi, blk[24:32], jnp.zeros((64, WIDTH), F32)], axis=0)
            tr.append(full.T)
            st.append(jnp.concatenate([s0, s1], axis=0).astype(BF))
            cadd.append(jnp.broadcast_to(centres[2 * b:2 * b + 1], (SLOTS, 256)))
            cadd.append(jnp.broadcast_to(centres[2 * b + 1:2 * b + 2], (SLOTS, 256)))
        stage(jnp.minimum(i + 1, ROWS // NB - 1))
        trans = jnp.concatenate(tr, axis=0)
        env1 = jnp.broadcast_to(trans[:, 56:57], (M, 128))
        env2 = jnp.concatenate([env1, env1], axis=1)
        tb = trans.astype(BF)
        sbd = tb[:, 0:32]
        h0 = (
            mm(cat(ghi, glo, ghi, tb), win_ref[...])
            + jnp.concatenate(cadd, axis=0)
        )
        a0, d0 = act(h0)
        lat0 = a0 * env2
        r0 = lat0.astype(BF)
        y0 = mm(r0, we0_ref[...])
        w0 = y0 * env2
        w0b = w0.astype(BF)

        def per_row(fn):
            return [fn(b, slice(b * WIDTH, (b + 1) * WIDTH)) for b in range(NB)]

        e0 = per_row(lambda b, s: mm(st[b], w0b[s]) * (1.0 / SLOTS))
        b0 = [(e * gmask).astype(BF) for e in e0]
        a_0 = jnp.concatenate(per_row(lambda b, s: mm(sbd[s], b0[b])), axis=0)
        sc0 = (w0 * a_0).astype(BF)
        h1 = mm(cat(r0, sc0), wl0_ref[...])
        a1, d1 = act(h1)
        lat1 = lat0 + a1
        r1 = lat1.astype(BF)
        y1 = mm(r1, we1_ref[...])
        w1b = (y1 * env2).astype(BF)
        e1 = per_row(lambda b, s: mm(st[b], w1b[s]) * (1.0 / SLOTS))
        b1 = [row0_of(e0[b]) * e1[b] * gmask + ksum(e0[b] * e1[b] * gmask) for b in range(NB)]
        b1 = [x.astype(BF) for x in b1]
        a_1 = jnp.concatenate(per_row(lambda b, s: mm(sbd[s], b1[b])), axis=0)
        sc1 = (w0 * a_1).astype(BF)
        h2 = mm(cat(r1, sc1), wl1_ref[...])
        a2, d2 = act(h2)
        wo = wout_ref[...]
        pq = (lat1 + a2) * wo
        pqh, pql = split2(pq[:, 0:128] + pq[:, 128:256])
        dlat2 = env2 * wo
        dz1 = (dlat2 * d2).astype(BF)
        dsc1 = mm(dz1, wl1t_ref[...])
        dw0 = dsc1 * a_1
        da1 = dsc1 * w0
        da1 = jnp.concatenate(
            [da1[:, 0:128].astype(BF), jnp.where(upper_m, w1b[:, 128:256].astype(F32), da1[:, 128:256]).astype(BF)], axis=1)
        db1 = per_row(lambda b, s: mm(st[b], da1[s]))
        de1, x0 = [], []
        for b in range(NB):
            head = row0_of(db1[b])
            prod = db1[b] * gmask
            de1.append(fold(gmask * head * e0[b] + prod * row0_of(e0[b])) * (1.0 / SLOTS))
            x0.append(gmask * head * e1[b] + ksum(prod * e1[b]))
        de1 = [jnp.where(upper, x, 0.0).astype(BF) for x in de1]
        b1c = [jnp.concatenate([b1[b][:, 0:128], (b1[b][:, 128:256].astype(F32) + de1[b].astype(F32)).astype(BF)], axis=1) for b in range(NB)]
        ds1 = per_row(lambda b, s: mm_nt(da1[s], b1c[b]))
        dw1 = jnp.concatenate(per_row(lambda b, s: mm(sbd[s], de1[b])), axis=0)
        ev = dw1 * y1[:, 128:256]
        dlat1 = dlat2 + mm(cat(dz1, (dw1 * env1).astype(BF)), lat1t_ref[...])
        dz0 = (dlat1 * d1).astype(BF)
        dsc0 = mm(dz0, wl0t_ref[...])
        dw0 = dw0 + dsc0 * a_0
        da0 = dsc0 * w0
        da0 = jnp.concatenate(
            [da0[:, 0:128].astype(BF), jnp.where(upper_m, w0[:, 128:256], da0[:, 128:256]).astype(BF)], axis=1)
        db0 = per_row(lambda b, s: mm(st[b], da0[s]))
        de0 = [jnp.where(upper, fold(x0[b] + gmask * db0[b]) * (1.0 / SLOTS), 0.0) for b in range(NB)]
        b0c = [jnp.concatenate([b0[b][:, 0:128], (b0[b][:, 128:256].astype(F32) + de0[b]).astype(BF)], axis=1) for b in range(NB)]
        ds = per_row(lambda b, s: ds1[b] + mm_nt(da0[s], b0c[b]))
        dw0e = jnp.concatenate(per_row(lambda b, s: mm(sbd[s], de0[b].astype(BF))), axis=0)
        dw0 = jnp.concatenate([dw0[:, 0:128], dw0[:, 128:256] + dw0e], axis=1)
        dlat0 = dlat1 + mm(cat(dz0, (dw0 * env2).astype(BF)), lat0t_ref[...])
        evl = dlat0 * a0 + dw0 * y0
        ev = ev + evl[:, 0:128] + evl[:, 128:256]
        evh, evo = split2(ev)
        dx0 = (dlat0 * env2 * d0).astype(BF)
        res = mm(cat(dx0, pqh, pql, evh, evo), rad_ref[...])
        for b in range(NB):
            dst = ds[b].T
            bgeo[i * NB + b, 0:16, :] = dst[0:16] * half0 + dst[16:32] * half1
            bgeo[i * NB + b, 16:32, :] = res[b * WIDTH:(b + 1) * WIDTH].T[0:16]
        return carry

    lax.fori_loop(0, ROWS // NB, chunk, 0)

    ux, uy, uz, inv, valid, poly, scaled, env, sins, coss = geometry(pos[0], pos[1], pos[2], idx_v[...])
    back = []
    for q in range(26):
        back.append(jnp.concatenate([bgeo[b, q:q + 1, :] for b in range(ROWS)], axis=0))
    gs, gb, q_e, denv = back[0:9], back[16:24], back[24], back[25]
    energy = env * q_e
    denv = denv + q_e
    dux = R3 * gs[1] + R15 * (uy * gs[4] + uz * gs[7] + ux * gs[8])
    duy = R3 * gs[2] + R15 * (ux * gs[4] + uz * gs[5] - uy * gs[8])
    duz = R3 * gs[3] + R15 * (uy * gs[5] + ux * gs[7]) + 3.0 * R5 * uz * gs[6]
    dd = denv * (valid * poly * scaled * (-4.0 / CUTOFF))
    for n in range(8):
        dd = dd + gb[n] * inv * (((n + 1) * math.pi / CUTOFF) * coss[n] - sins[n] * inv)
    dd = dd - (dux * ux + duy * uy + duz * uz) * inv
    dv = [dux * inv + dd * ux, duy * inv + dd * uy, duz * inv + dd * uz]

    for c in range(3):
        terms_ref[c] = dv[c]
    terms_ref[3] = energy
    for b in range(ROWS):
        placed_ref[pl.ds(slot_s[0, b], 1), :] = energy[b:b + 1]


def scatter_kernel(idx_v, terms_ref, left_ref, mid_ref, right_ref, ae_ref, lhs, rhs):
    safe = jnp.maximum(idx_v[...], 0)
    nhi = safe // 128
    nlo = safe - nhi * 128
    sub_h = lax.broadcasted_iota(jnp.int32, (HPAD, WIDTH), 0)
    sub_l = lax.broadcasted_iota(jnp.int32, (128, WIDTH), 0)
    sub_e = lax.broadcasted_iota(jnp.int32, (16, WIDTH), 0)
    half_i = lax.broadcasted_iota(jnp.int32, (128, WIDTH), 1) // SLOTS
    high = [terms_ref[c].astype(BF).astype(F32) for c in range(4)]
    low = [terms_ref[c] - high[c] for c in range(4)]
    for b in range(ROWS):
        cols = slice(b * WIDTH, (b + 1) * WIDTH)
        pick = sub_h == nhi[b:b + 1]
        parts = [jnp.where(pick, x[b:b + 1], 0.0) for x in high[:3] + low[:3]]
        parts.append(jnp.where(sub_e == 0, high[3][b:b + 1], jnp.where(sub_e == 1, low[3][b:b + 1], 0.0)))
        lhs[:, cols] = jnp.concatenate(parts, axis=0).astype(BF)
        one_lo = (sub_l == nlo[b:b + 1]).astype(F32)
        one_c = (sub_l == 2 * b + half_i).astype(F32)
        rhs[:, cols] = jnp.concatenate([one_lo, one_c], axis=0).astype(BF)
    acc = mm_nt(lhs[...], rhs[...])
    for c in range(3):
        both = acc[c * HPAD:(c + 1) * HPAD] + acc[(3 + c) * HPAD:(4 + c) * HPAD]
        centre = jnp.sum(both[:, 128:256], axis=0, keepdims=True)
        ghost = jnp.where(sub_h == 4 * 4, jnp.broadcast_to(centre, (HPAD, 128)), 0.0) - both[:, 0:128]
        left_ref[12 * c:12 * c + 12] = ghost[0:12]
        mid_ref[12 * c:12 * c + 12] = ghost[12:24]
        right_ref[12 * c:12 * c + 12] = ghost[24:36]
    ae_ref[...] = acc[240:241, 128:192] + acc[241:242, 128:192]


def local_terms(tables, pair_neighbor, offload_slot, cpart, weights):
    vm = pl.BlockSpec(memory_space=pltpu.VMEM)
    sm = pl.BlockSpec(memory_space=pltpu.SMEM)
    operands = [pair_neighbor, offload_slot, pair_neighbor, *tables, cpart, *weights]
    specs = [sm, sm] + [vm] * (len(operands) - 2)
    terms, placed = pl.pallas_call(
        kernel,
        out_shape=[
            jax.ShapeDtypeStruct((4, ROWS, WIDTH), F32),
            jax.ShapeDtypeStruct((ROWS, WIDTH), F32),
        ],
        in_specs=specs,
        out_specs=[vm] * 2,
        scratch_shapes=[
            pltpu.VMEM((LEAD + 9 * ATOMS, 128), F32),
            pltpu.VMEM((ROWS * WIDTH, 128), F32),
            pltpu.VMEM((3, ROWS, WIDTH), F32),
            pltpu.VMEM((ROWS, 32, WIDTH), F32),
            pltpu.VMEM((ROWS, 32, WIDTH), F32),
        ],
        compiler_params=pltpu.CompilerParams(vmem_limit_bytes=56 * 1024 * 1024),
        cost_estimate=pl.CostEstimate(flops=20_000_000_000, bytes_accessed=4_000_000, transcendentals=0),
    )(*operands)
    ghost = jax.ShapeDtypeStruct((36, 128), F32)
    left, mid, right, ae = pl.pallas_call(
        scatter_kernel,
        out_shape=[ghost, ghost, ghost, jax.ShapeDtypeStruct((1, 2 * ROWS), F32)],
        in_specs=[vm] * 2,
        out_specs=[vm] * 4,
        scratch_shapes=[pltpu.VMEM((256, ROWS * WIDTH), BF)] * 2,
        compiler_params=pltpu.CompilerParams(vmem_limit_bytes=24 * 1024 * 1024),
        cost_estimate=pl.CostEstimate(flops=5_000_000_000, bytes_accessed=1_000_000, transcendentals=0),
    )(pair_neighbor, terms)
    return left, mid, right, ae, placed


def prepare_kernel(
    feat, wc_ref, wn_ref, wr_ref, we_ref, wl_ref,
    cpart, win, we0, we1, wl0, wl1, wl0t, wl1t, lat0t, lat1t, rad,
):
    own = feat[:, 0:128].T[0:2 * ROWS]
    fhi, flo = split2(own)
    chi, clo = split2(0.5 * wc_ref[...])
    cpart[...] = mm(fhi, chi) + mm(flo, chi) + mm(fhi, clo)
    nhi, nlo = split2(0.5 * wn_ref[...])
    rhi, rlo = split2(0.5 * wr_ref[...])
    rhi, rlo = rhi.astype(F32), rlo.astype(F32)
    pad = jnp.zeros((64, 256), BF)
    radial = jnp.concatenate(
        [jnp.zeros((32, 256), F32), rhi, rhi, rlo, jnp.zeros((72, 256), F32)], axis=0)
    win[...] = jnp.concatenate([nhi, pad, nhi, pad, nlo, pad, radial.astype(BF)], axis=0)
    rt = jnp.concatenate([rhi, jnp.zeros((120, 256), F32)], axis=0).T
    lanes = lax.broadcasted_iota(jnp.int32, (256, 128), 1)
    rad[0:256] = rt.astype(BF)
    rad[256:512] = (lanes == 8).astype(F32).astype(BF)
    rad[512:768] = (lanes == 9).astype(F32).astype(BF)
    tile = (
        lax.broadcasted_iota(jnp.int32, (64, 256), 0)
        == lax.broadcasted_iota(jnp.int32, (64, 256), 1) % 64
    ).astype(F32).astype(BF)
    for layer, (we, wl, wlt, latt) in enumerate(
        ((we0, wl0, wl0t, lat0t), (we1, wl1, wl1t, lat1t))
    ):
        tiled = mm(we_ref[layer], tile)
        we[...] = tiled.astype(BF)
        halved = jnp.concatenate(
            [0.5 * wl_ref[layer].astype(F32), jnp.zeros((64, 256), F32)], axis=0)
        wl[...] = halved.astype(BF)
        wlt[...] = halved[256:512].T.astype(BF)
        latt[0:256] = halved[0:256].T.astype(BF)
        latt[256:] = tiled.T[0:latt.shape[0] - 256].astype(BF)


def prepare(atom_features, w_center, w_neigh, w_radial, w_env, w_latent, w_out):
    vm = pl.BlockSpec(memory_space=pltpu.VMEM)
    sd = jax.ShapeDtypeStruct
    sq = sd((256, 256), BF)
    shapes = [
        sd((2 * ROWS, 256), F32), sd((512, 256), BF), sq, sq, sd((512, 256), BF),
        sd((512, 256), BF), sq, sq, sd((512, 256), BF), sd((384, 256), BF), sd((768, 128), BF),
    ]
    cpart, *weights = pl.pallas_call(
        prepare_kernel,
        out_shape=shapes,
        in_specs=[vm] * 6,
        out_specs=[vm] * len(shapes),
        cost_estimate=pl.CostEstimate(flops=80_000_000, bytes_accessed=4_000_000, transcendentals=0),
    )(atom_features, w_center, w_neigh, w_radial, w_env, w_latent)
    return cpart, (*weights, w_out[None, :])


def per_device(
    positions, atom_features, pair_neighbor, offload_slot,
    w_center, w_neigh, w_radial, w_env, w_latent, w_out,
):
    def shift(x, axis, step):
        n = lax.axis_size(axis)
        return lax.ppermute(x, axis, [(i, (i + step) % n) for i in range(n)])

    own = jnp.concatenate([atom_features, positions], axis=0)
    col = [shift(own, "gy", 1), own, shift(own, "gy", -1)]
    left = [None, shift(own, "gx", 1), None]
    right = [None, shift(own, "gx", -1), None]
    for oy in (0, 2):
        left[oy] = shift(col[oy], "gx", 1)
        right[oy] = shift(col[oy], "gx", -1)
    cpart, weights = prepare(atom_features, w_center, w_neigh, w_radial, w_env, w_latent, w_out)
    g_left, g_mid, g_right, ae, placed = local_terms(
        left + col + right, pair_neighbor, offload_slot, cpart, weights)
    from_left = shift(g_right, "gx", 1)
    from_right = shift(g_left, "gx", -1)
    peers = lax.axis_size("gy")
    pair_energy = lax.all_to_all(
        placed.reshape(peers, ROWS // peers, WIDTH), "gy", split_axis=0, concat_axis=0, tiled=True
    ).reshape(ROWS, WIDTH)
    total = (g_mid + from_left + from_right).reshape(3, 3, 4, 128)
    up, down, pair_energy = lax.optimization_barrier((shift(total[:, 2], "gy", 1), shift(total[:, 0], "gy", -1), pair_energy))
    forces = total[:, 1] + up + down
    return forces.reshape(3, ATOMS), ae.reshape(2 * ROWS), pair_energy


def solution(mesh):
    spread = P(None, ("gx", "gy"))
    rows = P(("gx", "gy"), None)
    return jax.shard_map(
        per_device,
        mesh=mesh,
        in_specs=(spread, spread, rows, rows, P(), P(), P(), P(), P(), P()),
        out_specs=(spread, P(("gx", "gy")), rows),
        check_vma=False,
    )
```

```python
import math

import jax
import jax.numpy as jnp
from jax import lax
from jax.experimental import pallas as pl
from jax.experimental.pallas import tpu as pltpu
from jax.sharding import PartitionSpec as P

SOFTEN = 0.04
CUTOFF = 4.0
BF = jnp.bfloat16
F32 = jnp.float32
R3 = math.sqrt(3.0)
R5 = math.sqrt(5.0)
R15 = math.sqrt(15.0)
ROWS = 32
WIDTH = 128
SLOTS = 64
ATOMS = 512
NB = 8
M = NB * WIDTH
NT = (((1,), (1,)), ((), ()))
HPAD = 40
LEAD = 8


def mm(a, b):
    return jnp.dot(a, b, preferred_element_type=F32)


def cat(*xs):
    return jnp.concatenate(xs, axis=1)


def mm_nt(a, b):
    return lax.dot_general(a, b, NT, preferred_element_type=F32)


def split2(x):
    hi = x.astype(BF)
    return hi, (x - hi.astype(F32)).astype(BF)


def prepare_kernel(
    feat, wc_ref, wn_ref, wr_ref, we_ref, wl_ref,
    cpart, win, we0, we1, wl0, wl1, wl0t, wl1t, lat0t, lat1t, rad,
):
    own = feat[:, 0:128].T[0:2 * ROWS]
    fhi, flo = split2(own)
    chi, clo = split2(0.5 * wc_ref[...])
    cpart[...] = mm(fhi, chi) + mm(flo, chi) + mm(fhi, clo)
    nhi, nlo = split2(0.5 * wn_ref[...])
    rhi, rlo = split2(0.5 * wr_ref[...])
    rhi, rlo = rhi.astype(F32), rlo.astype(F32)
    pad = jnp.zeros((64, 256), BF)
    radial = jnp.concatenate(
        [jnp.zeros((32, 256), F32), rhi, rhi, rlo, jnp.zeros((72, 256), F32)], axis=0)
    win[...] = jnp.concatenate([nhi, pad, nhi, pad, nlo, pad, radial.astype(BF)], axis=0)
    rt = jnp.concatenate([rhi, jnp.zeros((120, 256), F32)], axis=0).T
    lanes = lax.broadcasted_iota(jnp.int32, (256, 128), 1)
    rad[0:256] = rt.astype(BF)
    rad[256:512] = (lanes == 8).astype(F32).astype(BF)
    rad[512:768] = (lanes == 9).astype(F32).astype(BF)
    tile = (
        lax.broadcasted_iota(jnp.int32, (64, 256), 0)
        == lax.broadcasted_iota(jnp.int32, (64, 256), 1) % 64
    ).astype(F32).astype(BF)
    for layer, (we, wl, wlt, latt) in enumerate(
        ((we0, wl0, wl0t, lat0t), (we1, wl1, wl1t, lat1t))
    ):
        tiled = mm(we_ref[layer], tile)
        we[...] = tiled.astype(BF)
        halved = jnp.concatenate(
            [0.5 * wl_ref[layer].astype(F32), jnp.zeros((64, 256), F32)], axis=0)
        wl[...] = halved.astype(BF)
        wlt[...] = halved[256:512].T.astype(BF)
        latt[0:256] = halved[0:256].T.astype(BF)
        latt[256:] = tiled.T[0:latt.shape[0] - 256].astype(BF)


def geometry(vx, vy, vz, index):
    valid = (index >= 0).astype(F32)
    dist = jnp.sqrt(vx * vx + vy * vy + vz * vz + SOFTEN)
    inv = 1.0 / dist
    scaled = dist * (1.0 / CUTOFF)
    poly = 1.0 - scaled * scaled
    env = valid * (poly * poly)
    theta = math.pi * scaled
    sins, coss = [jnp.sin(theta)], [jnp.cos(theta)]
    twice = 2.0 * coss[0]
    sprev, cprev = jnp.zeros_like(inv), jnp.ones_like(inv)
    for _ in range(7):
        snext = twice * sins[-1] - sprev
        cnext = twice * coss[-1] - cprev
        sprev, cprev = sins[-1], coss[-1]
        sins.append(snext)
        coss.append(cnext)
    return vx * inv, vy * inv, vz * inv, inv, valid, poly, scaled, env, sins, coss


def kernel(
    idx_s, slot_s, idx_v, t0, t1, t2, t3, t4, t5, t6, t7, t8,
    cpart, win_ref, we0_ref, we1_ref, wl0_ref, wl1_ref, wl0t_ref, wl1t_ref, lat0t_ref, lat1t_ref,
    rad_ref, wout_ref,
    left_ref, mid_ref, right_ref, ae_ref, placed_ref,
    table, gbuf, pos, geo, bgeo, lhs, rhs,
):
    tables = (t0, t1, t2, t3, t4, t5, t6, t7, t8)
    feats = 64
    table[0:LEAD, :] = jnp.zeros((LEAD, 128), F32)
    for o in range(9):
        ref = tables[o]
        shift = jnp.concatenate(
            [jnp.full((1, ATOMS), o // 3 - 1.0, F32), jnp.full((1, ATOMS), o % 3 - 1.0, F32),
             jnp.zeros((1, ATOMS), F32)], axis=0)
        posr = ref[feats:feats + 3, :] + shift
        for q in range(ATOMS // 128):
            block = jnp.concatenate(
                [ref[0:feats, q * 128:(q + 1) * 128], posr[:, q * 128:(q + 1) * 128],
                 jnp.zeros((61, 128), F32)], axis=0)
            table[pl.ds(LEAD + o * ATOMS + q * 128, 128), :] = block.T

    lane = lax.broadcasted_iota(jnp.int32, (NB, WIDTH), 1)
    row_i = lax.broadcasted_iota(jnp.int32, (NB, WIDTH), 0)
    own_t = table[pl.ds(LEAD + 4 * ATOMS, 128), :].T

    def stage(i):
        start = pl.multiple_of(i * M, M)
        for b in range(NB):
            for t in range(WIDTH):
                gbuf[pl.ds(start + (b * WIDTH + t), 1), :] = table[pl.ds(idx_s[i * NB + b, t] + LEAD, 1), :]
        turned = [gbuf[pl.ds(start + b * WIDTH, WIDTH), :].T for b in range(NB)]
        some = pl.ds(pl.multiple_of(i * NB, NB), NB)
        vec = []
        for c in range(3):
            end = jnp.concatenate([x[feats + c:feats + c + 1] for x in turned], axis=0)
            line = jnp.broadcast_to(own_t[feats + c:feats + c + 1, :], (NB, WIDTH))
            at = 2 * (row_i + i * NB)
            first = jnp.sum(jnp.where(lane == at, line, 0.0), axis=1, keepdims=True)
            second = jnp.sum(jnp.where(lane == at + 1, line, 0.0), axis=1, keepdims=True)
            vec.append(end - jnp.where(lane < SLOTS, first, second))
            pos[c, some, :] = vec[-1]
        ux, uy, uz, inv, _, _, _, env, sins, _ = geometry(*vec, idx_v[some, :])
        zero = jnp.zeros_like(ux)
        rows = [
            jnp.ones_like(ux), R3 * ux, R3 * uy, R3 * uz, R15 * ux * uy, R15 * uy * uz,
            0.5 * R5 * (3.0 * uz * uz - 1.0), R15 * ux * uz, 0.5 * R15 * (ux * ux - uy * uy),
        ] + [zero] * 7 + [x * inv for x in sins] + [env] + [zero] * 7
        for q in range(len(rows)):
            for b in range(NB):
                geo[i * NB + b, q:q + 1, :] = rows[q][b:b + 1, :]

    stage(0)

    lane_b = lax.broadcasted_iota(jnp.int32, (16, WIDTH), 1)
    half0 = (lane_b < SLOTS).astype(F32)
    half1 = 1.0 - half0
    kk = lax.broadcasted_iota(jnp.int32, (32, 256), 0) % 16
    gg = lax.broadcasted_iota(jnp.int32, (32, 256), 1) // 64
    group = jnp.where(kk == 0, 0, jnp.where(kk < 4, 1, jnp.where(kk < 9, 2, 4)))
    gmask = (group == gg).astype(F32)
    row0 = (kk == 0).astype(F32)
    upper = (lax.broadcasted_iota(jnp.int32, (32, 128), 1) >= 64)
    upper_m = lax.broadcasted_iota(jnp.int32, (M, 128), 1) >= 64
    first_row = lax.broadcasted_iota(jnp.int32, (32, 1), 0) < 16

    def row0_of(x):
        return jnp.concatenate(
            [jnp.broadcast_to(x[0:1], (16, x.shape[1])), jnp.broadcast_to(x[16:17], (16, x.shape[1]))], axis=0)

    def ksum(x):
        s0 = jnp.sum(x[0:16], axis=0, keepdims=True)
        s1 = jnp.sum(x[16:32], axis=0, keepdims=True)
        return jnp.concatenate(
            [jnp.broadcast_to(s0, (16, x.shape[1])), jnp.broadcast_to(s1, (16, x.shape[1]))], axis=0) * row0

    def fold(x):
        s = x[:, 0:128] + x[:, 128:256]
        return s + pltpu.roll(s, 64, 1)

    def act(h):
        t = jnp.tanh(h)
        u = 1.0 + t
        a = h * u
        return a, u + a * (1.0 - t)

    def chunk(i, carry):
        first = pl.multiple_of(i * M, M)
        g = gbuf[pl.ds(first, M), :]
        ghi, glo = split2(g)
        st, tr, cadd = [], [], []
        centres = cpart[pl.ds(pl.multiple_of(i * 2 * NB, 2 * NB), 2 * NB), :]
        for b in range(NB):
            blk = geo[i * NB + b]
            s0 = blk[0:16] * half0
            s1 = blk[0:16] * half1
            bas = blk[16:24]
            bhi = bas.astype(BF).astype(F32)
            full = jnp.concatenate(
                [s0, s1, bhi, bas - bhi, bhi, blk[24:32], jnp.zeros((64, WIDTH), F32)], axis=0)
            tr.append(full.T)
            st.append(jnp.concatenate([s0, s1], axis=0).astype(BF))
            cadd.append(jnp.broadcast_to(centres[2 * b:2 * b + 1], (SLOTS, 256)))
            cadd.append(jnp.broadcast_to(centres[2 * b + 1:2 * b + 2], (SLOTS, 256)))
        stage(jnp.minimum(i + 1, ROWS // NB - 1))
        trans = jnp.concatenate(tr, axis=0)
        env1 = jnp.broadcast_to(trans[:, 56:57], (M, 128))
        env2 = jnp.concatenate([env1, env1], axis=1)
        tb = trans.astype(BF)
        sbd = tb[:, 0:32]
        h0 = (
            mm(cat(ghi, glo, ghi, tb), win_ref[...])
            + jnp.concatenate(cadd, axis=0)
        )
        a0, d0 = act(h0)
        lat0 = a0 * env2
        r0 = lat0.astype(BF)
        y0 = mm(r0, we0_ref[...])
        w0 = y0 * env2
        w0b = w0.astype(BF)

        def per_row(fn):
            return [fn(b, slice(b * WIDTH, (b + 1) * WIDTH)) for b in range(NB)]

        e0 = per_row(lambda b, s: mm(st[b], w0b[s]) * (1.0 / SLOTS))
        b0 = [(e * gmask).astype(BF) for e in e0]
        a_0 = jnp.concatenate(per_row(lambda b, s: mm(sbd[s], b0[b])), axis=0)
        sc0 = (w0 * a_0).astype(BF)
        h1 = mm(cat(r0, sc0), wl0_ref[...])
        a1, d1 = act(h1)
        lat1 = lat0 + a1
        r1 = lat1.astype(BF)
        y1 = mm(r1, we1_ref[...])
        w1b = (y1 * env2).astype(BF)
        e1 = per_row(lambda b, s: mm(st[b], w1b[s]) * (1.0 / SLOTS))
        b1 = [row0_of(e0[b]) * e1[b] * gmask + ksum(e0[b] * e1[b] * gmask) for b in range(NB)]
        b1 = [x.astype(BF) for x in b1]
        a_1 = jnp.concatenate(per_row(lambda b, s: mm(sbd[s], b1[b])), axis=0)
        sc1 = (w0 * a_1).astype(BF)
        h2 = mm(cat(r1, sc1), wl1_ref[...])
        a2, d2 = act(h2)
        wo = wout_ref[...]
        pq = (lat1 + a2) * wo
        pqh, pql = split2(pq[:, 0:128] + pq[:, 128:256])
        dlat2 = env2 * wo
        dz1 = (dlat2 * d2).astype(BF)
        dsc1 = mm(dz1, wl1t_ref[...])
        dw0 = dsc1 * a_1
        da1 = dsc1 * w0
        da1 = jnp.concatenate(
            [da1[:, 0:128].astype(BF), jnp.where(upper_m, w1b[:, 128:256].astype(F32), da1[:, 128:256]).astype(BF)], axis=1)
        db1 = per_row(lambda b, s: mm(st[b], da1[s]))
        de1, x0 = [], []
        for b in range(NB):
            head = row0_of(db1[b])
            prod = db1[b] * gmask
            de1.append(fold(gmask * head * e0[b] + prod * row0_of(e0[b])) * (1.0 / SLOTS))
            x0.append(gmask * head * e1[b] + ksum(prod * e1[b]))
        de1 = [jnp.where(upper, x, 0.0).astype(BF) for x in de1]
        b1c = [jnp.concatenate([b1[b][:, 0:128], (b1[b][:, 128:256].astype(F32) + de1[b].astype(F32)).astype(BF)], axis=1) for b in range(NB)]
        ds1 = per_row(lambda b, s: mm_nt(da1[s], b1c[b]))
        dw1 = jnp.concatenate(per_row(lambda b, s: mm(sbd[s], de1[b])), axis=0)
        ev = dw1 * y1[:, 128:256]
        dlat1 = dlat2 + mm(cat(dz1, (dw1 * env1).astype(BF)), lat1t_ref[...])
        dz0 = (dlat1 * d1).astype(BF)
        dsc0 = mm(dz0, wl0t_ref[...])
        dw0 = dw0 + dsc0 * a_0
        da0 = dsc0 * w0
        da0 = jnp.concatenate(
            [da0[:, 0:128].astype(BF), jnp.where(upper_m, w0[:, 128:256], da0[:, 128:256]).astype(BF)], axis=1)
        db0 = per_row(lambda b, s: mm(st[b], da0[s]))
        de0 = [jnp.where(upper, fold(x0[b] + gmask * db0[b]) * (1.0 / SLOTS), 0.0) for b in range(NB)]
        b0c = [jnp.concatenate([b0[b][:, 0:128], (b0[b][:, 128:256].astype(F32) + de0[b]).astype(BF)], axis=1) for b in range(NB)]
        ds = per_row(lambda b, s: ds1[b] + mm_nt(da0[s], b0c[b]))
        dw0e = jnp.concatenate(per_row(lambda b, s: mm(sbd[s], de0[b].astype(BF))), axis=0)
        dw0 = jnp.concatenate([dw0[:, 0:128], dw0[:, 128:256] + dw0e], axis=1)
        dlat0 = dlat1 + mm(cat(dz0, (dw0 * env2).astype(BF)), lat0t_ref[...])
        evl = dlat0 * a0 + dw0 * y0
        ev = ev + evl[:, 0:128] + evl[:, 128:256]
        evh, evo = split2(ev)
        dx0 = (dlat0 * env2 * d0).astype(BF)
        res = mm(cat(dx0, pqh, pql, evh, evo), rad_ref[...])
        for b in range(NB):
            dst = ds[b].T
            bgeo[i * NB + b, 0:16, :] = dst[0:16] * half0 + dst[16:32] * half1
            bgeo[i * NB + b, 16:32, :] = res[b * WIDTH:(b + 1) * WIDTH].T[0:16]
        return carry

    lax.fori_loop(0, ROWS // NB, chunk, 0)

    ux, uy, uz, inv, valid, poly, scaled, env, sins, coss = geometry(pos[0], pos[1], pos[2], idx_v[...])
    back = []
    for q in range(26):
        back.append(jnp.concatenate([bgeo[b, q:q + 1, :] for b in range(ROWS)], axis=0))
    gs, gb, q_e, denv = back[0:9], back[16:24], back[24], back[25]
    energy = env * q_e
    denv = denv + q_e
    dux = R3 * gs[1] + R15 * (uy * gs[4] + uz * gs[7] + ux * gs[8])
    duy = R3 * gs[2] + R15 * (ux * gs[4] + uz * gs[5] - uy * gs[8])
    duz = R3 * gs[3] + R15 * (uy * gs[5] + ux * gs[7]) + 3.0 * R5 * uz * gs[6]
    dd = denv * (valid * poly * scaled * (-4.0 / CUTOFF))
    for n in range(8):
        dd = dd + gb[n] * inv * (((n + 1) * math.pi / CUTOFF) * coss[n] - sins[n] * inv)
    dd = dd - (dux * ux + duy * uy + duz * uz) * inv
    dv = [dux * inv + dd * ux, duy * inv + dd * uy, duz * inv + dd * uz]

    safe = jnp.maximum(idx_v[...], 0)
    nhi = safe // 128
    nlo = safe - nhi * 128
    sub_h = lax.broadcasted_iota(jnp.int32, (HPAD, WIDTH), 0)
    sub_l = lax.broadcasted_iota(jnp.int32, (128, WIDTH), 0)
    sub_e = lax.broadcasted_iota(jnp.int32, (16, WIDTH), 0)
    half_i = lax.broadcasted_iota(jnp.int32, (128, WIDTH), 1) // SLOTS
    terms = dv + [energy]
    high = [x.astype(BF).astype(F32) for x in terms]
    low = [x - y for x, y in zip(terms, high)]
    for b in range(ROWS):
        cols = slice(b * WIDTH, (b + 1) * WIDTH)
        pick = sub_h == nhi[b:b + 1]
        parts = [jnp.where(pick, x[b:b + 1], 0.0) for x in high[:3] + low[:3]]
        parts.append(jnp.where(sub_e == 0, high[3][b:b + 1], jnp.where(sub_e == 1, low[3][b:b + 1], 0.0)))
        lhs[:, cols] = jnp.concatenate(parts, axis=0).astype(BF)
        one_lo = (sub_l == nlo[b:b + 1]).astype(F32)
        one_c = (sub_l == 2 * b + half_i).astype(F32)
        rhs[:, cols] = jnp.concatenate([one_lo, one_c], axis=0).astype(BF)
        placed_ref[pl.ds(slot_s[0, b], 1), :] = energy[b:b + 1]
    acc = mm_nt(lhs[...], rhs[...])
    for c in range(3):
        both = acc[c * HPAD:(c + 1) * HPAD] + acc[(3 + c) * HPAD:(4 + c) * HPAD]
        centre = jnp.sum(both[:, 128:256], axis=0, keepdims=True)
        ghost = jnp.where(sub_h == 4 * 4, jnp.broadcast_to(centre, (HPAD, 128)), 0.0) - both[:, 0:128]
        left_ref[12 * c:12 * c + 12] = ghost[0:12]
        mid_ref[12 * c:12 * c + 12] = ghost[12:24]
        right_ref[12 * c:12 * c + 12] = ghost[24:36]
    ae_ref[...] = acc[240:241, 128:192] + acc[241:242, 128:192]


def local_terms(tables, pair_neighbor, offload_slot, weights):
    vm = pl.BlockSpec(memory_space=pltpu.VMEM)
    sm = pl.BlockSpec(memory_space=pltpu.SMEM)
    operands = [pair_neighbor, offload_slot, pair_neighbor, *tables, *weights]
    ghost = jax.ShapeDtypeStruct((36, 128), F32)
    return pl.pallas_call(
        kernel,
        out_shape=[
            ghost, ghost, ghost, jax.ShapeDtypeStruct((1, 2 * ROWS), F32),
            jax.ShapeDtypeStruct((ROWS, WIDTH), F32),
        ],
        in_specs=[sm, sm] + [vm] * (len(operands) - 2),
        out_specs=[vm] * 5,
        scratch_shapes=[
            pltpu.VMEM((LEAD + 9 * ATOMS, 128), F32),
            pltpu.VMEM((ROWS * WIDTH, 128), F32),
            pltpu.VMEM((3, ROWS, WIDTH), F32),
            pltpu.VMEM((ROWS, 32, WIDTH), F32),
            pltpu.VMEM((ROWS, 32, WIDTH), F32),
            pltpu.VMEM((256, ROWS * WIDTH), BF),
            pltpu.VMEM((256, ROWS * WIDTH), BF),
        ],
        compiler_params=pltpu.CompilerParams(vmem_limit_bytes=56 * 1024 * 1024),
        cost_estimate=pl.CostEstimate(flops=20_000_000_000, bytes_accessed=4_000_000, transcendentals=0),
    )(*operands)


def prepare(atom_features, w_center, w_neigh, w_radial, w_env, w_latent, w_out):
    vm = pl.BlockSpec(memory_space=pltpu.VMEM)
    sd = jax.ShapeDtypeStruct
    square, tall = sd((256, 256), BF), sd((512, 256), BF)
    shapes = [
        sd((2 * ROWS, 256), F32), tall, square, square, tall, tall, square, square, tall,
        sd((384, 256), BF), sd((768, 128), BF),
    ]
    weights = pl.pallas_call(
        prepare_kernel,
        out_shape=shapes,
        in_specs=[vm] * 6,
        out_specs=[vm] * len(shapes),
        cost_estimate=pl.CostEstimate(flops=80_000_000, bytes_accessed=4_000_000, transcendentals=0),
    )(atom_features, w_center, w_neigh, w_radial, w_env, w_latent)
    return (*weights, w_out[None, :])


def per_device(
    positions, atom_features, pair_neighbor, offload_slot,
    w_center, w_neigh, w_radial, w_env, w_latent, w_out,
):
    def shift(x, axis, step):
        n = lax.axis_size(axis)
        return lax.ppermute(x, axis, [(i, (i + step) % n) for i in range(n)])

    own = jnp.concatenate([atom_features, positions], axis=0)
    col = [shift(own, "gy", 1), own, shift(own, "gy", -1)]
    left = [None, shift(own, "gx", 1), None]
    right = [None, shift(own, "gx", -1), None]
    for oy in (0, 2):
        left[oy] = shift(col[oy], "gx", 1)
        right[oy] = shift(col[oy], "gx", -1)
    weights = prepare(atom_features, w_center, w_neigh, w_radial, w_env, w_latent, w_out)
    g_left, g_mid, g_right, ae, placed = local_terms(
        left + col + right, pair_neighbor, offload_slot, weights)
    from_left = shift(g_right, "gx", 1)
    from_right = shift(g_left, "gx", -1)
    pair_energy = lax.all_to_all(placed, "gy", split_axis=0, concat_axis=0, tiled=True)
    total = (g_mid + from_left + from_right).reshape(3, 3, 4, 128)
    up, down, pair_energy = lax.optimization_barrier((shift(total[:, 2], "gy", 1), shift(total[:, 0], "gy", -1), pair_energy))
    forces = total[:, 1] + up + down
    return forces.reshape(3, ATOMS), ae.reshape(2 * ROWS), pair_energy


def solution(mesh):
    spread = P(None, ("gx", "gy"))
    rows = P(("gx", "gy"), None)
    return jax.shard_map(
        per_device,
        mesh=mesh,
        in_specs=(spread, spread, rows, rows, P(), P(), P(), P(), P(), P()),
        out_specs=(spread, P(("gx", "gy")), rows),
        check_vma=False,
    )
```

```python
import math

import jax
import jax.numpy as jnp
from jax import lax
from jax.experimental import pallas as pl
from jax.experimental.pallas import tpu as pltpu
from jax.sharding import PartitionSpec as P

SOFTEN = 0.04
CUTOFF = 4.0
BF = jnp.bfloat16
F32 = jnp.float32
R3 = math.sqrt(3.0)
R5 = math.sqrt(5.0)
R15 = math.sqrt(15.0)
ROWS = 32
WIDTH = 128
SLOTS = 64
ATOMS = 512
NB = 8
M = NB * WIDTH
NT = (((1,), (1,)), ((), ()))
HPAD = 40
LEAD = 8


def mm(a, b):
    return jnp.dot(a, b, preferred_element_type=F32)


def cat(*xs):
    return jnp.concatenate(xs, axis=1)


def mm_nt(a, b):
    return lax.dot_general(a, b, NT, preferred_element_type=F32)


def split2(x):
    hi = x.astype(BF)
    return hi, (x - hi.astype(F32)).astype(BF)


def prepare_kernel(
    feat, wc_ref, wn_ref, wr_ref, we_ref, wl_ref,
    cpart, win, we0, we1, wl0, wl1, wl0t, wl1t, lat0t, lat1t, rad,
):
    own = feat[:, 0:128].T[0:2 * ROWS]
    fhi, flo = split2(own)
    chi, clo = split2(0.5 * wc_ref[...])
    cpart[...] = mm(fhi, chi) + mm(flo, chi) + mm(fhi, clo)
    rhi, rlo = split2(0.5 * wr_ref[...])
    rhi, rlo = rhi.astype(F32), rlo.astype(F32)
    pad = jnp.zeros((64, 256), BF)
    radial = jnp.concatenate(
        [jnp.zeros((32, 256), F32), rhi, rhi, rlo, jnp.zeros((72, 256), F32)], axis=0)
    win[...] = jnp.concatenate([(0.5 * wn_ref[...]).astype(BF), pad, radial.astype(BF)], axis=0)
    rt = jnp.concatenate([rhi, jnp.zeros((120, 256), F32)], axis=0).T
    lanes = lax.broadcasted_iota(jnp.int32, (256, 128), 1)
    rad[0:256] = rt.astype(BF)
    rad[256:512] = (lanes == 8).astype(F32).astype(BF)
    rad[512:768] = (lanes == 9).astype(F32).astype(BF)
    tile = (
        lax.broadcasted_iota(jnp.int32, (64, 256), 0)
        == lax.broadcasted_iota(jnp.int32, (64, 256), 1) % 64
    ).astype(F32).astype(BF)
    for layer, (we, wl, wlt, latt) in enumerate(
        ((we0, wl0, wl0t, lat0t), (we1, wl1, wl1t, lat1t))
    ):
        tiled = mm(we_ref[layer], tile)
        we[...] = tiled.astype(BF)
        halved = jnp.concatenate(
            [0.5 * wl_ref[layer].astype(F32), jnp.zeros((64, 256), F32)], axis=0)
        wl[...] = halved.astype(BF)
        wlt[...] = halved[256:512].T.astype(BF)
        latt[0:256] = halved[0:256].T.astype(BF)
        latt[256:] = tiled.T[0:latt.shape[0] - 256].astype(BF)


def geometry(vx, vy, vz, index):
    valid = (index >= 0).astype(F32)
    dist = jnp.sqrt(vx * vx + vy * vy + vz * vz + SOFTEN)
    inv = 1.0 / dist
    scaled = dist * (1.0 / CUTOFF)
    poly = 1.0 - scaled * scaled
    env = valid * (poly * poly)
    theta = math.pi * scaled
    sins, coss = [jnp.sin(theta)], [jnp.cos(theta)]
    twice = 2.0 * coss[0]
    sprev, cprev = jnp.zeros_like(inv), jnp.ones_like(inv)
    for _ in range(7):
        snext = twice * sins[-1] - sprev
        cnext = twice * coss[-1] - cprev
        sprev, cprev = sins[-1], coss[-1]
        sins.append(snext)
        coss.append(cnext)
    return vx * inv, vy * inv, vz * inv, inv, valid, poly, scaled, env, sins, coss


def kernel(
    idx_s, slot_s, idx_v, t0, t1, t2, t3, t4, t5, t6, t7, t8,
    cpart, win_ref, we0_ref, we1_ref, wl0_ref, wl1_ref, wl0t_ref, wl1t_ref, lat0t_ref, lat1t_ref,
    rad_ref, wout_ref,
    left_ref, mid_ref, right_ref, ae_ref, placed_ref,
    table, gbuf, pos, geo, bgeo, lhs, rhs,
):
    tables = (t0, t1, t2, t3, t4, t5, t6, t7, t8)
    feats = 64
    table[0:LEAD, :] = jnp.zeros((LEAD, 128), F32)
    for o in range(9):
        ref = tables[o]
        shift = jnp.concatenate(
            [jnp.full((1, ATOMS), o // 3 - 1.0, F32), jnp.full((1, ATOMS), o % 3 - 1.0, F32),
             jnp.zeros((1, ATOMS), F32)], axis=0)
        posr = ref[feats:feats + 3, :] + shift
        for q in range(ATOMS // 128):
            block = jnp.concatenate(
                [ref[0:feats, q * 128:(q + 1) * 128], posr[:, q * 128:(q + 1) * 128],
                 jnp.zeros((61, 128), F32)], axis=0)
            table[pl.ds(LEAD + o * ATOMS + q * 128, 128), :] = block.T

    lane = lax.broadcasted_iota(jnp.int32, (NB, WIDTH), 1)
    row_i = lax.broadcasted_iota(jnp.int32, (NB, WIDTH), 0)
    own_t = table[pl.ds(LEAD + 4 * ATOMS, 128), :].T

    def stage(i):
        start = pl.multiple_of(i * M, M)
        for b in range(NB):
            for t in range(WIDTH):
                gbuf[pl.ds(start + (b * WIDTH + t), 1), :] = table[pl.ds(idx_s[i * NB + b, t] + LEAD, 1), :]
        turned = [gbuf[pl.ds(start + b * WIDTH, WIDTH), :].T for b in range(NB)]
        some = pl.ds(pl.multiple_of(i * NB, NB), NB)
        vec = []
        for c in range(3):
            end = jnp.concatenate([x[feats + c:feats + c + 1] for x in turned], axis=0)
            line = jnp.broadcast_to(own_t[feats + c:feats + c + 1, :], (NB, WIDTH))
            at = 2 * (row_i + i * NB)
            first = jnp.sum(jnp.where(lane == at, line, 0.0), axis=1, keepdims=True)
            second = jnp.sum(jnp.where(lane == at + 1, line, 0.0), axis=1, keepdims=True)
            vec.append(end - jnp.where(lane < SLOTS, first, second))
            pos[c, some, :] = vec[-1]
        ux, uy, uz, inv, _, _, _, env, sins, _ = geometry(*vec, idx_v[some, :])
        zero = jnp.zeros_like(ux)
        rows = [
            jnp.ones_like(ux), R3 * ux, R3 * uy, R3 * uz, R15 * ux * uy, R15 * uy * uz,
            0.5 * R5 * (3.0 * uz * uz - 1.0), R15 * ux * uz, 0.5 * R15 * (ux * ux - uy * uy),
        ] + [zero] * 7 + [x * inv for x in sins] + [env] + [zero] * 7
        for q in range(len(rows)):
            for b in range(NB):
                geo[i * NB + b, q:q + 1, :] = rows[q][b:b + 1, :]

    stage(0)

    lane_b = lax.broadcasted_iota(jnp.int32, (16, WIDTH), 1)
    half0 = (lane_b < SLOTS).astype(F32)
    half1 = 1.0 - half0
    kk = lax.broadcasted_iota(jnp.int32, (32, 256), 0) % 16
    gg = lax.broadcasted_iota(jnp.int32, (32, 256), 1) // 64
    group = jnp.where(kk == 0, 0, jnp.where(kk < 4, 1, jnp.where(kk < 9, 2, 4)))
    gmask = (group == gg).astype(F32)
    row0 = (kk == 0).astype(F32)
    upper = (lax.broadcasted_iota(jnp.int32, (32, 128), 1) >= 64)
    upper_m = lax.broadcasted_iota(jnp.int32, (M, 128), 1) >= 64
    first_row = lax.broadcasted_iota(jnp.int32, (32, 1), 0) < 16

    def row0_of(x):
        return jnp.concatenate(
            [jnp.broadcast_to(x[0:1], (16, x.shape[1])), jnp.broadcast_to(x[16:17], (16, x.shape[1]))], axis=0)

    def ksum(x):
        s0 = jnp.sum(x[0:16], axis=0, keepdims=True)
        s1 = jnp.sum(x[16:32], axis=0, keepdims=True)
        return jnp.concatenate(
            [jnp.broadcast_to(s0, (16, x.shape[1])), jnp.broadcast_to(s1, (16, x.shape[1]))], axis=0) * row0

    def fold(x):
        s = x[:, 0:128] + x[:, 128:256]
        return s + pltpu.roll(s, 64, 1)

    def act(h):
        t = jnp.tanh(h)
        u = 1.0 + t
        a = h * u
        return a, u + a * (1.0 - t)

    def chunk(i, carry):
        first = pl.multiple_of(i * M, M)
        g = gbuf[pl.ds(first, M), :]
        ghi = g.astype(BF)
        st, tr, cadd = [], [], []
        centres = cpart[pl.ds(pl.multiple_of(i * 2 * NB, 2 * NB), 2 * NB), :]
        for b in range(NB):
            blk = geo[i * NB + b]
            s0 = blk[0:16] * half0
            s1 = blk[0:16] * half1
            bas = blk[16:24]
            bhi = bas.astype(BF).astype(F32)
            full = jnp.concatenate(
                [s0, s1, bhi, bas - bhi, bhi, blk[24:32], jnp.zeros((64, WIDTH), F32)], axis=0)
            tr.append(full.T)
            st.append(jnp.concatenate([s0, s1], axis=0).astype(BF))
            cadd.append(jnp.broadcast_to(centres[2 * b:2 * b + 1], (SLOTS, 256)))
            cadd.append(jnp.broadcast_to(centres[2 * b + 1:2 * b + 2], (SLOTS, 256)))
        stage(jnp.minimum(i + 1, ROWS // NB - 1))
        trans = jnp.concatenate(tr, axis=0)
        env1 = jnp.broadcast_to(trans[:, 56:57], (M, 128))
        env2 = jnp.concatenate([env1, env1], axis=1)
        tb = trans.astype(BF)
        sbd = tb[:, 0:32]
        h0 = (
            mm(cat(ghi, tb), win_ref[...])
            + jnp.concatenate(cadd, axis=0)
        )
        a0, d0 = act(h0)
        lat0 = a0 * env2
        r0 = lat0.astype(BF)
        y0 = mm(r0, we0_ref[...])
        w0 = y0 * env2
        w0b = w0.astype(BF)

        def per_row(fn):
            return [fn(b, slice(b * WIDTH, (b + 1) * WIDTH)) for b in range(NB)]

        e0 = per_row(lambda b, s: mm(st[b], w0b[s]) * (1.0 / SLOTS))
        b0 = [(e * gmask).astype(BF) for e in e0]
        a_0 = jnp.concatenate(per_row(lambda b, s: mm(sbd[s], b0[b])), axis=0)
        sc0 = (w0 * a_0).astype(BF)
        h1 = mm(cat(r0, sc0), wl0_ref[...])
        a1, d1 = act(h1)
        lat1 = lat0 + a1
        r1 = lat1.astype(BF)
        y1 = mm(r1, we1_ref[...])
        w1b = (y1 * env2).astype(BF)
        e1 = per_row(lambda b, s: mm(st[b], w1b[s]) * (1.0 / SLOTS))
        b1 = [row0_of(e0[b]) * e1[b] * gmask + ksum(e0[b] * e1[b] * gmask) for b in range(NB)]
        b1 = [x.astype(BF) for x in b1]
        a_1 = jnp.concatenate(per_row(lambda b, s: mm(sbd[s], b1[b])), axis=0)
        sc1 = (w0 * a_1).astype(BF)
        h2 = mm(cat(r1, sc1), wl1_ref[...])
        a2, d2 = act(h2)
        wo = wout_ref[...]
        pq = (lat1 + a2) * wo
        pqh, pql = split2(pq[:, 0:128] + pq[:, 128:256])
        dlat2 = env2 * wo
        dz1 = (dlat2 * d2).astype(BF)
        dsc1 = mm(dz1, wl1t_ref[...])
        dw0 = dsc1 * a_1
        da1 = dsc1 * w0
        da1 = jnp.concatenate(
            [da1[:, 0:128].astype(BF), jnp.where(upper_m, w1b[:, 128:256].astype(F32), da1[:, 128:256]).astype(BF)], axis=1)
        db1 = per_row(lambda b, s: mm(st[b], da1[s]))
        de1, x0 = [], []
        for b in range(NB):
            head = row0_of(db1[b])
            prod = db1[b] * gmask
            de1.append(fold(gmask * head * e0[b] + prod * row0_of(e0[b])) * (1.0 / SLOTS))
            x0.append(gmask * head * e1[b] + ksum(prod * e1[b]))
        de1 = [jnp.where(upper, x, 0.0).astype(BF) for x in de1]
        b1c = [jnp.concatenate([b1[b][:, 0:128], (b1[b][:, 128:256].astype(F32) + de1[b].astype(F32)).astype(BF)], axis=1) for b in range(NB)]
        ds1 = per_row(lambda b, s: mm_nt(da1[s], b1c[b]))
        dw1 = jnp.concatenate(per_row(lambda b, s: mm(sbd[s], de1[b])), axis=0)
        ev = dw1 * y1[:, 128:256]
        dlat1 = dlat2 + mm(cat(dz1, (dw1 * env1).astype(BF)), lat1t_ref[...])
        dz0 = (dlat1 * d1).astype(BF)
        dsc0 = mm(dz0, wl0t_ref[...])
        dw0 = dw0 + dsc0 * a_0
        da0 = dsc0 * w0
        da0 = jnp.concatenate(
            [da0[:, 0:128].astype(BF), jnp.where(upper_m, w0[:, 128:256], da0[:, 128:256]).astype(BF)], axis=1)
        db0 = per_row(lambda b, s: mm(st[b], da0[s]))
        de0 = [jnp.where(upper, fold(x0[b] + gmask * db0[b]) * (1.0 / SLOTS), 0.0) for b in range(NB)]
        b0c = [jnp.concatenate([b0[b][:, 0:128], (b0[b][:, 128:256].astype(F32) + de0[b]).astype(BF)], axis=1) for b in range(NB)]
        ds = per_row(lambda b, s: ds1[b] + mm_nt(da0[s], b0c[b]))
        dw0e = jnp.concatenate(per_row(lambda b, s: mm(sbd[s], de0[b].astype(BF))), axis=0)
        dw0 = jnp.concatenate([dw0[:, 0:128], dw0[:, 128:256] + dw0e], axis=1)
        dlat0 = dlat1 + mm(cat(dz0, (dw0 * env2).astype(BF)), lat0t_ref[...])
        evl = dlat0 * a0 + dw0 * y0
        ev = ev + evl[:, 0:128] + evl[:, 128:256]
        evh, evo = split2(ev)
        dx0 = (dlat0 * env2 * d0).astype(BF)
        res = mm(cat(dx0, pqh, pql, evh, evo), rad_ref[...])
        for b in range(NB):
            dst = ds[b].T
            bgeo[i * NB + b, 0:16, :] = dst[0:16] * half0 + dst[16:32] * half1
            bgeo[i * NB + b, 16:32, :] = res[b * WIDTH:(b + 1) * WIDTH].T[0:16]
        return carry

    lax.fori_loop(0, ROWS // NB, chunk, 0)

    ux, uy, uz, inv, valid, poly, scaled, env, sins, coss = geometry(pos[0], pos[1], pos[2], idx_v[...])
    back = []
    for q in range(26):
        back.append(jnp.concatenate([bgeo[b, q:q + 1, :] for b in range(ROWS)], axis=0))
    gs, gb, q_e, denv = back[0:9], back[16:24], back[24], back[25]
    energy = env * q_e
    denv = denv + q_e
    dux = R3 * gs[1] + R15 * (uy * gs[4] + uz * gs[7] + ux * gs[8])
    duy = R3 * gs[2] + R15 * (ux * gs[4] + uz * gs[5] - uy * gs[8])
    duz = R3 * gs[3] + R15 * (uy * gs[5] + ux * gs[7]) + 3.0 * R5 * uz * gs[6]
    dd = denv * (valid * poly * scaled * (-4.0 / CUTOFF))
    for n in range(8):
        dd = dd + gb[n] * inv * (((n + 1) * math.pi / CUTOFF) * coss[n] - sins[n] * inv)
    dd = dd - (dux * ux + duy * uy + duz * uz) * inv
    dv = [dux * inv + dd * ux, duy * inv + dd * uy, duz * inv + dd * uz]

    safe = jnp.maximum(idx_v[...], 0)
    nhi = safe // 128
    nlo = safe - nhi * 128
    sub_h = lax.broadcasted_iota(jnp.int32, (HPAD, WIDTH), 0)
    sub_l = lax.broadcasted_iota(jnp.int32, (128, WIDTH), 0)
    sub_e = lax.broadcasted_iota(jnp.int32, (16, WIDTH), 0)
    half_i = lax.broadcasted_iota(jnp.int32, (128, WIDTH), 1) // SLOTS
    terms = dv + [energy]
    high = [x.astype(BF).astype(F32) for x in terms]
    low = [x - y for x, y in zip(terms, high)]
    for b in range(ROWS):
        cols = slice(b * WIDTH, (b + 1) * WIDTH)
        pick = sub_h == nhi[b:b + 1]
        parts = [jnp.where(pick, x[b:b + 1], 0.0) for x in high[:3] + low[:3]]
        parts.append(jnp.where(sub_e == 0, high[3][b:b + 1], jnp.where(sub_e == 1, low[3][b:b + 1], 0.0)))
        lhs[:, cols] = jnp.concatenate(parts, axis=0).astype(BF)
        one_lo = (sub_l == nlo[b:b + 1]).astype(F32)
        one_c = (sub_l == 2 * b + half_i).astype(F32)
        rhs[:, cols] = jnp.concatenate([one_lo, one_c], axis=0).astype(BF)
        placed_ref[pl.ds(slot_s[0, b], 1), :] = energy[b:b + 1]
    acc = mm_nt(lhs[...], rhs[...])
    for c in range(3):
        both = acc[c * HPAD:(c + 1) * HPAD] + acc[(3 + c) * HPAD:(4 + c) * HPAD]
        centre = jnp.sum(both[:, 128:256], axis=0, keepdims=True)
        ghost = jnp.where(sub_h == 4 * 4, jnp.broadcast_to(centre, (HPAD, 128)), 0.0) - both[:, 0:128]
        left_ref[12 * c:12 * c + 12] = ghost[0:12]
        mid_ref[12 * c:12 * c + 12] = ghost[12:24]
        right_ref[12 * c:12 * c + 12] = ghost[24:36]
    ae_ref[...] = acc[240:241, 128:192] + acc[241:242, 128:192]


def local_terms(tables, pair_neighbor, offload_slot, weights):
    vm = pl.BlockSpec(memory_space=pltpu.VMEM)
    sm = pl.BlockSpec(memory_space=pltpu.SMEM)
    operands = [pair_neighbor, offload_slot, pair_neighbor, *tables, *weights]
    ghost = jax.ShapeDtypeStruct((36, 128), F32)
    return pl.pallas_call(
        kernel,
        out_shape=[
            ghost, ghost, ghost, jax.ShapeDtypeStruct((1, 2 * ROWS), F32),
            jax.ShapeDtypeStruct((ROWS, WIDTH), F32),
        ],
        in_specs=[sm, sm] + [vm] * (len(operands) - 2),
        out_specs=[vm] * 5,
        scratch_shapes=[
            pltpu.VMEM((LEAD + 9 * ATOMS, 128), F32),
            pltpu.VMEM((ROWS * WIDTH, 128), F32),
            pltpu.VMEM((3, ROWS, WIDTH), F32),
            pltpu.VMEM((ROWS, 32, WIDTH), F32),
            pltpu.VMEM((ROWS, 32, WIDTH), F32),
            pltpu.VMEM((256, ROWS * WIDTH), BF),
            pltpu.VMEM((256, ROWS * WIDTH), BF),
        ],
        compiler_params=pltpu.CompilerParams(vmem_limit_bytes=56 * 1024 * 1024),
        cost_estimate=pl.CostEstimate(flops=20_000_000_000, bytes_accessed=4_000_000, transcendentals=0),
    )(*operands)


def prepare(atom_features, w_center, w_neigh, w_radial, w_env, w_latent, w_out):
    vm = pl.BlockSpec(memory_space=pltpu.VMEM)
    sd = jax.ShapeDtypeStruct
    square, tall = sd((256, 256), BF), sd((512, 256), BF)
    shapes = [
        sd((2 * ROWS, 256), F32), square, square, square, tall, tall, square, square, tall,
        sd((384, 256), BF), sd((768, 128), BF),
    ]
    weights = pl.pallas_call(
        prepare_kernel,
        out_shape=shapes,
        in_specs=[vm] * 6,
        out_specs=[vm] * len(shapes),
        cost_estimate=pl.CostEstimate(flops=80_000_000, bytes_accessed=4_000_000, transcendentals=0),
    )(atom_features, w_center, w_neigh, w_radial, w_env, w_latent)
    return (*weights, w_out[None, :])


def per_device(
    positions, atom_features, pair_neighbor, offload_slot,
    w_center, w_neigh, w_radial, w_env, w_latent, w_out,
):
    def shift(x, axis, step):
        n = lax.axis_size(axis)
        return lax.ppermute(x, axis, [(i, (i + step) % n) for i in range(n)])

    own = jnp.concatenate([atom_features, positions], axis=0)
    col = [shift(own, "gy", 1), own, shift(own, "gy", -1)]
    left = [None, shift(own, "gx", 1), None]
    right = [None, shift(own, "gx", -1), None]
    for oy in (0, 2):
        left[oy] = shift(col[oy], "gx", 1)
        right[oy] = shift(col[oy], "gx", -1)
    weights = prepare(atom_features, w_center, w_neigh, w_radial, w_env, w_latent, w_out)
    g_left, g_mid, g_right, ae, placed = local_terms(
        left + col + right, pair_neighbor, offload_slot, weights)
    from_left = shift(g_right, "gx", 1)
    from_right = shift(g_left, "gx", -1)
    pair_energy = lax.all_to_all(placed, "gy", split_axis=0, concat_axis=0, tiled=True)
    total = (g_mid + from_left + from_right).reshape(3, 3, 4, 128)
    up, down, pair_energy = lax.optimization_barrier((shift(total[:, 2], "gy", 1), shift(total[:, 0], "gy", -1), pair_energy))
    forces = total[:, 1] + up + down
    return forces.reshape(3, ATOMS), ae.reshape(2 * ROWS), pair_energy


def solution(mesh):
    spread = P(None, ("gx", "gy"))
    rows = P(("gx", "gy"), None)
    return jax.shard_map(
        per_device,
        mesh=mesh,
        in_specs=(spread, spread, rows, rows, P(), P(), P(), P(), P(), P()),
        out_specs=(spread, P(("gx", "gy")), rows),
        check_vma=False,
    )
```

```python
import math

import jax
import jax.numpy as jnp
from jax import lax
from jax.experimental import pallas as pl
from jax.experimental.pallas import tpu as pltpu
from jax.sharding import PartitionSpec as P

SOFTEN = 0.04
CUTOFF = 4.0
BF = jnp.bfloat16
F32 = jnp.float32
R3 = math.sqrt(3.0)
R5 = math.sqrt(5.0)
R15 = math.sqrt(15.0)
ROWS = 32
WIDTH = 128
SLOTS = 64
ATOMS = 512
NB = 8
M = NB * WIDTH
NT = (((1,), (1,)), ((), ()))
HPAD = 40
LEAD = 8


def mm(a, b):
    return jnp.dot(a, b, preferred_element_type=F32)


def cat(*xs):
    return jnp.concatenate(xs, axis=1)


def mm_nt(a, b):
    return lax.dot_general(a, b, NT, preferred_element_type=F32)


def split2(x):
    hi = x.astype(BF)
    return hi, (x - hi.astype(F32)).astype(BF)


def prepare_kernel(
    feat, wc_ref, wn_ref, wr_ref, we_ref, wl_ref,
    cpart, win, we0, we1, wl0, wl1, wl0t, wl1t, lat0t, lat1t, rad,
):
    own = feat[:, 0:128].T[0:2 * ROWS]
    fhi, flo = split2(own)
    chi, clo = split2(0.5 * wc_ref[...])
    cpart[...] = mm(fhi, chi) + mm(flo, chi) + mm(fhi, clo)
    rhi, rlo = split2(0.5 * wr_ref[...])
    rhi, rlo = rhi.astype(F32), rlo.astype(F32)
    pad = jnp.zeros((64, 256), BF)
    radial = jnp.concatenate(
        [jnp.zeros((32, 256), F32), rhi, rhi, rlo, jnp.zeros((72, 256), F32)], axis=0)
    win[...] = jnp.concatenate([(0.5 * wn_ref[...]).astype(BF), pad, radial.astype(BF)], axis=0)
    rt = jnp.concatenate([rhi, jnp.zeros((120, 256), F32)], axis=0).T
    lanes = lax.broadcasted_iota(jnp.int32, (128, 128), 1)
    rad[0:256] = rt.astype(BF)
    rad[256:384] = (lanes == 8).astype(F32).astype(BF)
    rad[384:512] = (lanes == 9).astype(F32).astype(BF)
    tile = (
        lax.broadcasted_iota(jnp.int32, (64, 256), 0)
        == lax.broadcasted_iota(jnp.int32, (64, 256), 1) % 64
    ).astype(F32).astype(BF)
    for layer, (we, wl, wlt, latt) in enumerate(
        ((we0, wl0, wl0t, lat0t), (we1, wl1, wl1t, lat1t))
    ):
        tiled = mm(we_ref[layer], tile)
        we[...] = tiled.astype(BF)
        halved = jnp.concatenate(
            [0.5 * wl_ref[layer].astype(F32), jnp.zeros((64, 256), F32)], axis=0)
        wl[...] = halved.astype(BF)
        wlt[...] = halved[256:512].T.astype(BF)
        latt[0:256] = halved[0:256].T.astype(BF)
        latt[256:] = tiled.T[0:latt.shape[0] - 256].astype(BF)


def geometry(vx, vy, vz, index):
    valid = (index >= 0).astype(F32)
    dist = jnp.sqrt(vx * vx + vy * vy + vz * vz + SOFTEN)
    inv = 1.0 / dist
    scaled = dist * (1.0 / CUTOFF)
    poly = 1.0 - scaled * scaled
    env = valid * (poly * poly)
    theta = math.pi * scaled
    sins, coss = [jnp.sin(theta)], [jnp.cos(theta)]
    twice = 2.0 * coss[0]
    sprev, cprev = jnp.zeros_like(inv), jnp.ones_like(inv)
    for _ in range(7):
        snext = twice * sins[-1] - sprev
        cnext = twice * coss[-1] - cprev
        sprev, cprev = sins[-1], coss[-1]
        sins.append(snext)
        coss.append(cnext)
    return vx * inv, vy * inv, vz * inv, inv, valid, poly, scaled, env, sins, coss


def kernel(
    idx_s, slot_s, idx_v, t0, t1, t2, t3, t4, t5, t6, t7, t8,
    cpart, win_ref, we0_ref, we1_ref, wl0_ref, wl1_ref, wl0t_ref, wl1t_ref, lat0t_ref, lat1t_ref,
    rad_ref, wout_ref,
    left_ref, mid_ref, right_ref, ae_ref, placed_ref,
    table, gbuf, pos, geo, bgeo, lhs, rhs,
):
    tables = (t0, t1, t2, t3, t4, t5, t6, t7, t8)
    feats = 64
    table[0:LEAD, :] = jnp.zeros((LEAD, 128), F32)
    for o in range(9):
        ref = tables[o]
        shift = jnp.concatenate(
            [jnp.full((1, ATOMS), o // 3 - 1.0, F32), jnp.full((1, ATOMS), o % 3 - 1.0, F32),
             jnp.zeros((1, ATOMS), F32)], axis=0)
        posr = ref[feats:feats + 3, :] + shift
        for q in range(ATOMS // 128):
            block = jnp.concatenate(
                [ref[0:feats, q * 128:(q + 1) * 128], posr[:, q * 128:(q + 1) * 128],
                 jnp.zeros((61, 128), F32)], axis=0)
            table[pl.ds(LEAD + o * ATOMS + q * 128, 128), :] = block.T

    lane = lax.broadcasted_iota(jnp.int32, (NB, WIDTH), 1)
    row_i = lax.broadcasted_iota(jnp.int32, (NB, WIDTH), 0)
    own_t = table[pl.ds(LEAD + 4 * ATOMS, 128), :].T

    def stage(i):
        start = pl.multiple_of(i * M, M)
        for b in range(NB):
            for t in range(WIDTH):
                gbuf[pl.ds(start + (b * WIDTH + t), 1), :] = table[pl.ds(idx_s[i * NB + b, t] + LEAD, 1), :]
        turned = [gbuf[pl.ds(start + b * WIDTH, WIDTH), :].T for b in range(NB)]
        some = pl.ds(pl.multiple_of(i * NB, NB), NB)
        vec = []
        for c in range(3):
            end = jnp.concatenate([x[feats + c:feats + c + 1] for x in turned], axis=0)
            line = jnp.broadcast_to(own_t[feats + c:feats + c + 1, :], (NB, WIDTH))
            at = 2 * (row_i + i * NB)
            first = jnp.sum(jnp.where(lane == at, line, 0.0), axis=1, keepdims=True)
            second = jnp.sum(jnp.where(lane == at + 1, line, 0.0), axis=1, keepdims=True)
            vec.append(end - jnp.where(lane < SLOTS, first, second))
            pos[c, some, :] = vec[-1]
        ux, uy, uz, inv, _, _, _, env, sins, _ = geometry(*vec, idx_v[some, :])
        zero = jnp.zeros_like(ux)
        rows = [
            jnp.ones_like(ux), R3 * ux, R3 * uy, R3 * uz, R15 * ux * uy, R15 * uy * uz,
            0.5 * R5 * (3.0 * uz * uz - 1.0), R15 * ux * uz, 0.5 * R15 * (ux * ux - uy * uy),
        ] + [zero] * 7 + [x * inv for x in sins] + [env] + [zero] * 7
        for q in range(len(rows)):
            for b in range(NB):
                geo[i * NB + b, q:q + 1, :] = rows[q][b:b + 1, :]

    stage(0)

    lane_b = lax.broadcasted_iota(jnp.int32, (16, WIDTH), 1)
    half0 = (lane_b < SLOTS).astype(F32)
    half1 = 1.0 - half0
    kk = lax.broadcasted_iota(jnp.int32, (32, 256), 0) % 16
    gg = lax.broadcasted_iota(jnp.int32, (32, 256), 1) // 64
    group = jnp.where(kk == 0, 0, jnp.where(kk < 4, 1, jnp.where(kk < 9, 2, 4)))
    gmask = (group == gg).astype(F32)
    row0 = (kk == 0).astype(F32)
    upper = (lax.broadcasted_iota(jnp.int32, (32, 128), 1) >= 64)
    upper_m = lax.broadcasted_iota(jnp.int32, (M, 128), 1) >= 64
    first_row = lax.broadcasted_iota(jnp.int32, (32, 1), 0) < 16

    def row0_of(x):
        return jnp.concatenate(
            [jnp.broadcast_to(x[0:1], (16, x.shape[1])), jnp.broadcast_to(x[16:17], (16, x.shape[1]))], axis=0)

    def ksum(x):
        s0 = jnp.sum(x[0:16], axis=0, keepdims=True)
        s1 = jnp.sum(x[16:32], axis=0, keepdims=True)
        return jnp.concatenate(
            [jnp.broadcast_to(s0, (16, x.shape[1])), jnp.broadcast_to(s1, (16, x.shape[1]))], axis=0) * row0

    def fold(x):
        s = x[:, 0:128] + x[:, 128:256]
        return s + pltpu.roll(s, 64, 1)

    def act(h):
        t = jnp.tanh(h)
        u = 1.0 + t
        a = h * u
        return a, u + a * (1.0 - t)

    def chunk(i, carry):
        first = pl.multiple_of(i * M, M)
        g = gbuf[pl.ds(first, M), :]
        ghi = g.astype(BF)
        st, tr, cadd = [], [], []
        centres = cpart[pl.ds(pl.multiple_of(i * 2 * NB, 2 * NB), 2 * NB), :]
        for b in range(NB):
            blk = geo[i * NB + b]
            s0 = blk[0:16] * half0
            s1 = blk[0:16] * half1
            bas = blk[16:24]
            bhi = bas.astype(BF).astype(F32)
            full = jnp.concatenate(
                [s0, s1, bhi, bas - bhi, bhi, blk[24:32], jnp.zeros((64, WIDTH), F32)], axis=0)
            tr.append(full.T)
            st.append(jnp.concatenate([s0, s1], axis=0).astype(BF))
            cadd.append(jnp.broadcast_to(centres[2 * b:2 * b + 1], (SLOTS, 256)))
            cadd.append(jnp.broadcast_to(centres[2 * b + 1:2 * b + 2], (SLOTS, 256)))
        stage(jnp.minimum(i + 1, ROWS // NB - 1))
        trans = jnp.concatenate(tr, axis=0)
        env1 = jnp.broadcast_to(trans[:, 56:57], (M, 128))
        env2 = jnp.concatenate([env1, env1], axis=1)
        tb = trans.astype(BF)
        sbd = tb[:, 0:32]
        h0 = (
            mm(cat(ghi, tb), win_ref[...])
            + jnp.concatenate(cadd, axis=0)
        )
        a0, d0 = act(h0)
        lat0 = a0 * env2
        r0 = lat0.astype(BF)
        y0 = mm(r0, we0_ref[...])
        w0 = y0 * env2
        w0b = w0.astype(BF)

        def per_row(fn):
            return [fn(b, slice(b * WIDTH, (b + 1) * WIDTH)) for b in range(NB)]

        e0 = per_row(lambda b, s: mm(st[b], w0b[s]) * (1.0 / SLOTS))
        b0 = [(e * gmask).astype(BF) for e in e0]
        a_0 = jnp.concatenate(per_row(lambda b, s: mm(sbd[s], b0[b])), axis=0)
        sc0 = (w0 * a_0).astype(BF)
        h1 = mm(cat(r0, sc0), wl0_ref[...])
        a1, d1 = act(h1)
        lat1 = lat0 + a1
        r1 = lat1.astype(BF)
        y1 = mm(r1, we1_ref[...])
        w1b = (y1 * env2).astype(BF)
        e1 = per_row(lambda b, s: mm(st[b], w1b[s]) * (1.0 / SLOTS))
        b1 = [row0_of(e0[b]) * e1[b] * gmask + ksum(e0[b] * e1[b] * gmask) for b in range(NB)]
        b1 = [x.astype(BF) for x in b1]
        a_1 = jnp.concatenate(per_row(lambda b, s: mm(sbd[s], b1[b])), axis=0)
        sc1 = (w0 * a_1).astype(BF)
        h2 = mm(cat(r1, sc1), wl1_ref[...])
        a2, d2 = act(h2)
        wo = wout_ref[...]
        pq = (lat1 + a2) * wo
        pqh = (pq[:, 0:128] + pq[:, 128:256]).astype(BF)
        dlat2 = env2 * wo
        dz1 = (dlat2 * d2).astype(BF)
        dsc1 = mm(dz1, wl1t_ref[...])
        dw0 = dsc1 * a_1
        da1 = dsc1 * w0
        da1 = jnp.concatenate(
            [da1[:, 0:128].astype(BF), jnp.where(upper_m, w1b[:, 128:256].astype(F32), da1[:, 128:256]).astype(BF)], axis=1)
        db1 = per_row(lambda b, s: mm(st[b], da1[s]))
        de1, x0 = [], []
        for b in range(NB):
            head = row0_of(db1[b])
            prod = db1[b] * gmask
            de1.append(fold(gmask * head * e0[b] + prod * row0_of(e0[b])) * (1.0 / SLOTS))
            x0.append(gmask * head * e1[b] + ksum(prod * e1[b]))
        de1 = [jnp.where(upper, x, 0.0).astype(BF) for x in de1]
        b1c = [jnp.concatenate([b1[b][:, 0:128], (b1[b][:, 128:256].astype(F32) + de1[b].astype(F32)).astype(BF)], axis=1) for b in range(NB)]
        ds1 = per_row(lambda b, s: mm_nt(da1[s], b1c[b]))
        dw1 = jnp.concatenate(per_row(lambda b, s: mm(sbd[s], de1[b])), axis=0)
        ev = dw1 * y1[:, 128:256]
        dlat1 = dlat2 + mm(cat(dz1, (dw1 * env1).astype(BF)), lat1t_ref[...])
        dz0 = (dlat1 * d1).astype(BF)
        dsc0 = mm(dz0, wl0t_ref[...])
        dw0 = dw0 + dsc0 * a_0
        da0 = dsc0 * w0
        da0 = jnp.concatenate(
            [da0[:, 0:128].astype(BF), jnp.where(upper_m, w0[:, 128:256], da0[:, 128:256]).astype(BF)], axis=1)
        db0 = per_row(lambda b, s: mm(st[b], da0[s]))
        de0 = [jnp.where(upper, fold(x0[b] + gmask * db0[b]) * (1.0 / SLOTS), 0.0) for b in range(NB)]
        b0c = [jnp.concatenate([b0[b][:, 0:128], (b0[b][:, 128:256].astype(F32) + de0[b]).astype(BF)], axis=1) for b in range(NB)]
        ds = per_row(lambda b, s: ds1[b] + mm_nt(da0[s], b0c[b]))
        dw0e = jnp.concatenate(per_row(lambda b, s: mm(sbd[s], de0[b].astype(BF))), axis=0)
        dw0 = jnp.concatenate([dw0[:, 0:128], dw0[:, 128:256] + dw0e], axis=1)
        dlat0 = dlat1 + mm(cat(dz0, (dw0 * env2).astype(BF)), lat0t_ref[...])
        evl = dlat0 * a0 + dw0 * y0
        ev = ev + evl[:, 0:128] + evl[:, 128:256]
        evh = ev.astype(BF)
        dx0 = (dlat0 * env2 * d0).astype(BF)
        res = mm(cat(dx0, pqh, evh), rad_ref[...])
        for b in range(NB):
            dst = ds[b].T
            bgeo[i * NB + b, 0:16, :] = dst[0:16] * half0 + dst[16:32] * half1
            bgeo[i * NB + b, 16:32, :] = res[b * WIDTH:(b + 1) * WIDTH].T[0:16]
        return carry

    lax.fori_loop(0, ROWS // NB, chunk, 0)

    ux, uy, uz, inv, valid, poly, scaled, env, sins, coss = geometry(pos[0], pos[1], pos[2], idx_v[...])
    back = []
    for q in range(26):
        back.append(jnp.concatenate([bgeo[b, q:q + 1, :] for b in range(ROWS)], axis=0))
    gs, gb, q_e, denv = back[0:9], back[16:24], back[24], back[25]
    energy = env * q_e
    denv = denv + q_e
    dux = R3 * gs[1] + R15 * (uy * gs[4] + uz * gs[7] + ux * gs[8])
    duy = R3 * gs[2] + R15 * (ux * gs[4] + uz * gs[5] - uy * gs[8])
    duz = R3 * gs[3] + R15 * (uy * gs[5] + ux * gs[7]) + 3.0 * R5 * uz * gs[6]
    dd = denv * (valid * poly * scaled * (-4.0 / CUTOFF))
    for n in range(8):
        dd = dd + gb[n] * inv * (((n + 1) * math.pi / CUTOFF) * coss[n] - sins[n] * inv)
    dd = dd - (dux * ux + duy * uy + duz * uz) * inv
    dv = [dux * inv + dd * ux, duy * inv + dd * uy, duz * inv + dd * uz]

    safe = jnp.maximum(idx_v[...], 0)
    nhi = safe // 128
    nlo = safe - nhi * 128
    sub_h = lax.broadcasted_iota(jnp.int32, (HPAD, WIDTH), 0)
    sub_l = lax.broadcasted_iota(jnp.int32, (128, WIDTH), 0)
    sub_e = lax.broadcasted_iota(jnp.int32, (16, WIDTH), 0)
    half_i = lax.broadcasted_iota(jnp.int32, (128, WIDTH), 1) // SLOTS
    terms = dv + [energy]
    high = [x.astype(BF).astype(F32) for x in terms]
    low = [x - y for x, y in zip(terms, high)]
    for b in range(ROWS):
        cols = slice(b * WIDTH, (b + 1) * WIDTH)
        pick = sub_h == nhi[b:b + 1]
        parts = [jnp.where(pick, x[b:b + 1], 0.0) for x in high[:3] + low[:3]]
        parts.append(jnp.where(sub_e == 0, high[3][b:b + 1], jnp.where(sub_e == 1, low[3][b:b + 1], 0.0)))
        lhs[:, cols] = jnp.concatenate(parts, axis=0).astype(BF)
        one_lo = (sub_l == nlo[b:b + 1]).astype(F32)
        one_c = (sub_l == 2 * b + half_i).astype(F32)
        rhs[:, cols] = jnp.concatenate([one_lo, one_c], axis=0).astype(BF)
        placed_ref[pl.ds(slot_s[0, b], 1), :] = energy[b:b + 1]
    acc = mm_nt(lhs[...], rhs[...])
    for c in range(3):
        both = acc[c * HPAD:(c + 1) * HPAD] + acc[(3 + c) * HPAD:(4 + c) * HPAD]
        centre = jnp.sum(both[:, 128:256], axis=0, keepdims=True)
        ghost = jnp.where(sub_h == 4 * 4, jnp.broadcast_to(centre, (HPAD, 128)), 0.0) - both[:, 0:128]
        left_ref[12 * c:12 * c + 12] = ghost[0:12]
        mid_ref[12 * c:12 * c + 12] = ghost[12:24]
        right_ref[12 * c:12 * c + 12] = ghost[24:36]
    ae_ref[...] = acc[240:241, 128:192] + acc[241:242, 128:192]


def local_terms(tables, pair_neighbor, offload_slot, weights):
    vm = pl.BlockSpec(memory_space=pltpu.VMEM)
    sm = pl.BlockSpec(memory_space=pltpu.SMEM)
    operands = [pair_neighbor, offload_slot, pair_neighbor, *tables, *weights]
    ghost = jax.ShapeDtypeStruct((36, 128), F32)
    return pl.pallas_call(
        kernel,
        out_shape=[
            ghost, ghost, ghost, jax.ShapeDtypeStruct((1, 2 * ROWS), F32),
            jax.ShapeDtypeStruct((ROWS, WIDTH), F32),
        ],
        in_specs=[sm, sm] + [vm] * (len(operands) - 2),
        out_specs=[vm] * 5,
        scratch_shapes=[
            pltpu.VMEM((LEAD + 9 * ATOMS, 128), F32),
            pltpu.VMEM((ROWS * WIDTH, 128), F32),
            pltpu.VMEM((3, ROWS, WIDTH), F32),
            pltpu.VMEM((ROWS, 32, WIDTH), F32),
            pltpu.VMEM((ROWS, 32, WIDTH), F32),
            pltpu.VMEM((256, ROWS * WIDTH), BF),
            pltpu.VMEM((256, ROWS * WIDTH), BF),
        ],
        compiler_params=pltpu.CompilerParams(vmem_limit_bytes=56 * 1024 * 1024),
        cost_estimate=pl.CostEstimate(flops=20_000_000_000, bytes_accessed=4_000_000, transcendentals=0),
    )(*operands)


def prepare(atom_features, w_center, w_neigh, w_radial, w_env, w_latent, w_out):
    vm = pl.BlockSpec(memory_space=pltpu.VMEM)
    sd = jax.ShapeDtypeStruct
    square, tall = sd((256, 256), BF), sd((512, 256), BF)
    shapes = [
        sd((2 * ROWS, 256), F32), square, square, square, tall, tall, square, square, tall,
        sd((384, 256), BF), sd((512, 128), BF),
    ]
    weights = pl.pallas_call(
        prepare_kernel,
        out_shape=shapes,
        in_specs=[vm] * 6,
        out_specs=[vm] * len(shapes),
        cost_estimate=pl.CostEstimate(flops=80_000_000, bytes_accessed=4_000_000, transcendentals=0),
    )(atom_features, w_center, w_neigh, w_radial, w_env, w_latent)
    return (*weights, w_out[None, :])


def per_device(
    positions, atom_features, pair_neighbor, offload_slot,
    w_center, w_neigh, w_radial, w_env, w_latent, w_out,
):
    def shift(x, axis, step):
        n = lax.axis_size(axis)
        return lax.ppermute(x, axis, [(i, (i + step) % n) for i in range(n)])

    own = jnp.concatenate([atom_features, positions], axis=0)
    col = [shift(own, "gy", 1), own, shift(own, "gy", -1)]
    left = [None, shift(own, "gx", 1), None]
    right = [None, shift(own, "gx", -1), None]
    for oy in (0, 2):
        left[oy] = shift(col[oy], "gx", 1)
        right[oy] = shift(col[oy], "gx", -1)
    weights = prepare(atom_features, w_center, w_neigh, w_radial, w_env, w_latent, w_out)
    g_left, g_mid, g_right, ae, placed = local_terms(
        left + col + right, pair_neighbor, offload_slot, weights)
    from_left = shift(g_right, "gx", 1)
    from_right = shift(g_left, "gx", -1)
    pair_energy = lax.all_to_all(placed, "gy", split_axis=0, concat_axis=0, tiled=True)
    total = (g_mid + from_left + from_right).reshape(3, 3, 4, 128)
    up, down, pair_energy = lax.optimization_barrier((shift(total[:, 2], "gy", 1), shift(total[:, 0], "gy", -1), pair_energy))
    forces = total[:, 1] + up + down
    return forces.reshape(3, ATOMS), ae.reshape(2 * ROWS), pair_energy


def solution(mesh):
    spread = P(None, ("gx", "gy"))
    rows = P(("gx", "gy"), None)
    return jax.shard_map(
        per_device,
        mesh=mesh,
        in_specs=(spread, spread, rows, rows, P(), P(), P(), P(), P(), P()),
        out_specs=(spread, P(("gx", "gy")), rows),
        check_vma=False,
    )
```
